32 devices in a mesh: space: 8 (over z, y), fsdp: 4 (over x, core).
Axes of the slice: x: 2, y: 2, z: 4, core: 2. Of those that a mesh axis runs over, the one named last changes fastest.
Arguments:
- fields: bfloat16 [16, 64, 64, 200], P('space', 'fsdp'), may hold values from -6 to 6
- weight: bfloat16 [5, 5, 40, 200], P(None, None, None, 'fsdp'), may hold values from -0.1875 to 0.1875
- bias: bfloat16 [200], P('fsdp'), may hold values from -3 to 3
- cotangent: bfloat16 [16, 64, 64, 200], P('space', 'fsdp'), may hold values from -9 to 9
- neighbours: int32 [16, 8], P('space'), may hold values from -1 to 15, as said below
Outputs:
- activations: bfloat16 [16, 64, 64, 200], P('space', 'fsdp')
- weight_step: float32 [5, 5, 40, 200], P(None, None, None, 'fsdp')
- bias_step: float32 [200], P('fsdp')
The draws below stay inside these ranges and needn't reach their ends.
Inputs may be any that keep to these rules, and one draw needn't show every extreme that they name: The tiles are the ocean tiles of a region 4 tiles tall, numbered column by column from west to east and north to south within a column, land tiles skipped; neighbours[t, k] is the tile beside t in direction k, or -1 where that place is land or outside the region; every neighbour differs from t by at most 5.
All inputs are finite; a program needn't handle non-finite values.
Results may differ from the reference program's by a relative error of at most 0.0034.
Values may be sent and summed in bfloat16 or wider, within the bound.
No kernel may reach another device: no remote copies, remote signals or barrier semaphores. Data moves between devices by JAX's collectives and lax.ppermute only.
A program may use at most 64 MiB of HBM per device.

```python
import jax
import jax.numpy as jnp
from jax import lax

C = 200
GROUP = 40
KS = 5
TILE = 64
BAND = 4
TILES = 16


def draw_neighbours(key, part):
    column_count = (TILES + TILES // 4) // BAND
    place_count = column_count * BAND
    land_count = place_count - TILES
    order = jax.random.permutation(key, place_count)
    land = jnp.zeros((place_count,), jnp.int32).at[order[:land_count]].set(1)
    ocean = 1 - land
    slot_ids = jnp.cumsum(ocean) - 1
    slot_ids = jnp.where(ocean == 1, slot_ids, -1).astype(jnp.int32)
    grid = slot_ids.reshape(column_count, BAND)
    framed = jnp.full((column_count + 2, BAND + 2), -1, jnp.int32).at[1:-1, 1:-1].set(grid)
    moves = [(-1, 0), (1, 0), (0, -1), (0, 1), (-1, -1), (-1, 1), (1, -1), (1, 1)]
    lists = [framed[1 + col_step:1 + col_step + column_count, 1 + row_step:1 + row_step + BAND] for row_step, col_step in moves]
    table = jnp.stack(lists, -1).reshape(place_count, 8)
    target = jnp.where(ocean == 1, slot_ids, TILES)
    return jnp.full((TILES, 8), -1, jnp.int32).at[target].set(table, mode='drop')


def draw_cotangent(key, part):
    ramp = jnp.arange(C, dtype=jnp.float32) / (C - 1)
    base = jnp.clip(jax.random.normal(key, (TILES, TILE, TILE, C), jnp.float32), -5.0, 5.0)
    spread = jnp.exp(ramp * 0.5 * jnp.log(3.0))
    return (base * spread).astype(jnp.bfloat16)


def levels(stream_key, dims, cuts, least, top_value):
    factor_of = 1.0
    for dim, parts in cuts:
        heights = jax.random.uniform(jax.random.fold_in(jax.random.fold_in(stream_key, 6), dim), (parts,), jnp.float32, least / len(cuts), top_value / len(cuts))
        factor_of = factor_of * jnp.repeat(jnp.exp(heights), dims[dim] // parts).reshape((-1,) + (1,) * (len(dims) - 1 - dim))
    return factor_of


def scatter_about(rng, extent, scale, most, pieces=(), kind=jnp.bfloat16):
    gain = levels(rng, extent, pieces, -0.22, 0.18) if pieces else 1.0
    result = jax.random.normal(rng, extent, jnp.float32) * scale * gain
    return jnp.minimum(jnp.maximum(result, -most), most).astype(kind)


def setup_inputs(seed: int = 0) -> dict:
    arg_keys = jax.random.split(jax.random.key(seed), 6)
    fields = scatter_about(arg_keys[0], (TILES, TILE, TILE, C), 1.0, 6.0, ((0, 8), (1, 4)))
    weight = scatter_about(arg_keys[1], (KS, KS, GROUP, C), (KS * KS * GROUP) ** -0.5, 0.1875, ((3, 4),))
    bias = scatter_about(arg_keys[2], (C,), 0.5, 3.0, ((0, 4),))
    cotangent = draw_cotangent(jax.random.fold_in(arg_keys[5], 71), 0)
    neighbours = draw_neighbours(jax.random.fold_in(arg_keys[5], 71), 0)
    return {"fields": fields, "weight": weight, "bias": bias, "cotangent": cotangent, "neighbours": neighbours}


def neighbourhood(extended, near_ids, centre):
    rim_width = KS // 2
    beside_all = [extended[near_ids[direction]] for direction in range(8)]
    north_tile, south_tile, west_tile, east_tile = (beside_all[0], beside_all[1], beside_all[2], beside_all[3])
    north_west, north_east, south_west, south_east = (beside_all[4], beside_all[5], beside_all[6], beside_all[7])
    top_band = jnp.concatenate([north_west[-rim_width:, -rim_width:], north_tile[-rim_width:], north_east[-rim_width:, :rim_width]], 1)
    middle = jnp.concatenate([west_tile[:, -rim_width:], centre, east_tile[:, :rim_width]], 1)
    bottom = jnp.concatenate([south_west[:rim_width, -rim_width:], south_tile[:rim_width], south_east[:rim_width, :rim_width]], 1)
    return jnp.concatenate([top_band, middle, bottom], 0)

def convolve(padded, kernel_arg):
    return lax.conv_general_dilated(padded, kernel_arg, (1, 1), 'VALID', dimension_numbers=('NHWC', 'HWIO', 'NHWC'), feature_group_count=C // GROUP)

def reference(fields, weight, bias, cotangent, neighbours):
    zero_tile = jnp.zeros((1, TILE, TILE, C), fields.dtype)
    extended = jnp.concatenate([fields, zero_tile], 0)
    near_all = jnp.where(neighbours < 0, TILES, neighbours).astype(jnp.int32)
    kernel = weight.astype(jnp.float32)
    bias_wide = bias.astype(jnp.float32)
    block_size = 16

    def block_section(start):
        tile_ids = start + jnp.arange(block_size, dtype=jnp.int32)
        padded = jax.vmap(lambda tile_id: neighbourhood(extended, near_all[tile_id], extended[tile_id]))(tile_ids)
        padded = padded.astype(jnp.float32)
        preact = convolve(padded, kernel) + bias_wide
        logistic = jax.nn.sigmoid(preact)
        activated = (preact * logistic).astype(jnp.bfloat16)
        upstream = lax.dynamic_slice_in_dim(cotangent, start, block_size, 0).astype(jnp.float32)
        pre_grad = (upstream * logistic * (1.0 + preact * (1.0 - logistic))).astype(jnp.bfloat16)
        pre_grad = lax.optimization_barrier(pre_grad).astype(jnp.float32)
        unused, pullback = jax.vjp(lambda kernel_arg: convolve(padded, kernel_arg), kernel)
        weight_grad = pullback(pre_grad)[0]
        bias_grad = lax.optimization_barrier(jnp.sum(pre_grad, axis=(0, 1, 2)))
        return (activated, weight_grad, bias_grad)
    block_starts = jnp.arange(TILES // block_size, dtype=jnp.int32) * block_size
    activated_all, weight_parts, bias_parts = lax.map(block_section, block_starts)
    weight_grad = lax.optimization_barrier(jnp.sum(weight_parts, 0))
    bias_grad = lax.optimization_barrier(jnp.sum(bias_parts, 0))
    mean_square = (jnp.sum(weight_grad * weight_grad) + jnp.sum(bias_grad * bias_grad)) / (KS * KS * GROUP * C + C)
    scaling = lax.rsqrt(mean_square + 1e-06)
    return (activated_all.reshape(TILES, TILE, TILE, C), weight_grad * scaling, bias_grad * scaling)
```

```python
import functools

import jax
import jax.numpy as jnp
from jax import lax
from jax.experimental import pallas as pl
from jax.experimental.pallas import tpu as pltpu
from jax.sharding import PartitionSpec as P

GROUP = 40
KS = 5
RIM = 2
LANES = 256
HALF = 64
HALF_TAPS = 13
PIECE_ROWS = 528
SUM_LANES = 1024
XROWS = 208
VMEM = pl.BlockSpec(memory_space=pltpu.VMEM)
SMEM = pl.BlockSpec(memory_space=pltpu.SMEM)
F32 = jnp.float32
BF16 = jnp.bfloat16


def swapped(value, axis, partner):
    count = lax.axis_size(axis)
    pairs = [(i, partner(i)) for i in range(count)]
    return lax.ppermute(value, axis, [p for p in pairs if 0 <= p[1] < count])


def hop_pairs(value, distance, parity):
    def partner(i):
        return i + distance if (i // distance) % 2 == parity else i - distance

    return swapped(value, "space", partner)


def main_kernel(
    piece_count, near, fields, cot, above, below, far0, far1, close0, close1, edge0, edge1, *rest
):
    pieces = rest[:piece_count]
    act, keep, send = rest[piece_count : piece_count + 3]
    pool_l, pool_r, xf, xs, xst, wc, wd, g, gd, shares = rest[piece_count + 3 :]
    tiles, rows, side, chans = fields.shape
    tall = rows + 2 * RIM
    cells = tiles * side
    fsdp_count = lax.axis_size("fsdp")
    fsdp = lax.axis_index("fsdp")
    space = lax.axis_index("space")
    far_odd = lax.rem(lax.div(space, 2), 2) == 1
    close_odd = lax.rem(space, 2) == 1
    share = chans // fsdp_count

    zero_side = jnp.zeros((tall, RIM, LANES), F32)
    zero_slot = 4 * tiles
    pool_l[zero_slot] = zero_side
    pool_r[zero_slot] = zero_side
    for t in range(tiles):
        lo, hi = far0[t].astype(F32), far1[t].astype(F32)
        pool_l[tiles + t, :, :, :chans] = jnp.where(far_odd, lo, hi)
        pool_r[2 * tiles + t, :, :, :chans] = jnp.where(far_odd, hi, lo)
        lo = close0[t * tall : (t + 1) * tall].astype(F32)
        hi = close1[t * tall : (t + 1) * tall].astype(F32)
        pool_l[2 * tiles + t, :, :, :chans] = jnp.where(close_odd, lo, hi)
        pool_r[tiles + t, :, :, :chans] = jnp.where(close_odd, hi, lo)
    lo = close0[tiles * tall :].astype(F32)
    hi = close1[tiles * tall :].astype(F32)
    pool_l[tiles - 1, :RIM, :, :chans] = jnp.where(close_odd, lo, hi)
    pool_r[3 * tiles, rows + RIM :, :, :chans] = jnp.where(close_odd, hi, lo)
    lo, hi = edge0[...].astype(F32), edge1[...].astype(F32)
    edge_north = jnp.where(close_odd, lo, hi)
    edge_south = jnp.where(close_odd, hi, lo)

    lane = lax.broadcasted_iota(jnp.int32, (tiles, side + 16, 128), 2)
    one_behind = jnp.where(lane == chans - 128, 1.0, 0.0).astype(F32)
    for r in range(tall):
        xf[r, :, :, 128:] = one_behind
    for t in range(tiles):
        top, bottom = above[t].astype(F32), below[t].astype(F32)
        centre = fields[t].astype(F32)
        for part, first in ((top, 0), (centre, RIM), (bottom, RIM + rows)):
            length = part.shape[0]
            pool_l[3 * tiles + t, first : first + length, :, :chans] = part[:, side - RIM :]
            pool_r[t, first : first + length, :, :chans] = part[:, :RIM]
        xf[RIM : RIM + rows, t, 8 : 8 + side, :chans] = centre
        north = edge_north if t == 0 else above[t - 1].astype(F32)
        south = edge_south if t == tiles - 1 else below[t + 1].astype(F32)
        north = jnp.where(near[t, 0] >= 0, north, 0.0)
        south = jnp.where(near[t, 1] >= 0, south, 0.0)
        xf[:RIM, t, 8 : 8 + side, :chans] = jnp.where(fsdp == 0, north, top)
        xf[RIM + rows :, t, 8 : 8 + side, :chans] = jnp.where(fsdp == fsdp_count - 1, south, bottom)

    def slot(tile_id, first):
        return jnp.where(tile_id < 0, zero_slot, jnp.clip(tile_id - first * tiles, 0, zero_slot))

    for t in range(tiles):
        for pool, column, first, beside, up, down in (
            (pool_l, 6, space - 3, near[t, 2], near[t, 4], near[t, 6]),
            (pool_r, 8 + side, space, near[t, 3], near[t, 5], near[t, 7]),
        ):
            mid = slot(beside, first)
            top = jnp.where(fsdp == 0, slot(up, first), mid)
            bottom = jnp.where(fsdp == fsdp_count - 1, slot(down, first), mid)
            into = pl.ds(column, RIM)
            xf[RIM : RIM + rows, t, into, :chans] = pool[mid, RIM : RIM + rows, :, :chans]
            xf[:RIM, t, into, :chans] = pool[top, :RIM, :, :chans]
            xf[RIM + rows :, t, into, :chans] = pool[bottom, RIM + rows :, :, :chans]

    lined = jnp.concatenate([p[...] for p in pieces], axis=1)
    owner = []
    for i in range(piece_count):
        if piece_count == fsdp_count and fsdp_count != 4:
            owner.append(i)
        else:
            owner.append((fsdp, 3 - fsdp, fsdp ^ 1, 3 - (fsdp ^ 1))[i])
    from_lane = lax.broadcasted_iota(jnp.int32, (128, LANES), 0)
    to_lane = lax.broadcasted_iota(jnp.int32, (128, LANES), 1)
    for half in range(2):
        picks = []
        for i in range(piece_count):
            inside = from_lane - half * HALF
            valid = (inside >= 0) & (inside < share) & (to_lane == owner[i] * share + inside)
            picks.append(jnp.where(valid, 1.0, 0.0).astype(BF16))
        full = jnp.dot(lined, jnp.concatenate(picks, axis=0), preferred_element_type=F32)
        wc[half * HALF_TAPS * GROUP : (half + 1) * HALF_TAPS * GROUP, :] = full[: HALF_TAPS * GROUP]
    group_count = chans // GROUP
    group_of = lax.broadcasted_iota(jnp.int32, (GROUP, LANES), 1) // GROUP
    taps = KS * KS
    for tap in range(taps):
        one = wc[tap * GROUP : (tap + 1) * GROUP]
        blocks = [jnp.where(group_of == k, one, 0.0) for k in range(group_count)]
        if tap == taps // 2:
            blocks.append(wc[taps * GROUP : taps * GROUP + 8])
        else:
            blocks.append(jnp.zeros((8, LANES), F32))
        blocks.append(jnp.zeros((LANES - chans - 8, LANES), F32))
        wd[tap * LANES : (tap + 1) * LANES] = jnp.concatenate(blocks, axis=0).astype(BF16)

    @pl.loop(0, tall)
    def _(r):
        for b in range(KS):
            piece = xf[r, :, 6 + b : 6 + b + side, :].astype(BF16).reshape(cells, LANES)
            xs[r, :, b * LANES : (b + 1) * LANES] = piece
            xst[r, b * XROWS : (b + 1) * XROWS, :] = piece.T[:XROWS]

    step = min(8, rows)
    for r0 in range(0, rows, step):
        total = None
        for a in range(KS):
            left = xs[r0 + a : r0 + a + step].reshape(step * cells, KS * LANES)
            right = wd[a * KS * LANES : (a + 1) * KS * LANES]
            part = jnp.dot(left, right, preferred_element_type=F32)
            total = part if total is None else total + part
        total = total.reshape(step, tiles, side, LANES)
        for t in range(tiles):
            pre = total[:, t, :, :chans]
            logistic = 1.0 / (1.0 + jnp.exp(-pre))
            act[t, r0 : r0 + step] = (pre * logistic).astype(BF16)
            up = cot[t, r0 : r0 + step].astype(F32)
            g[r0 : r0 + step, t * side : (t + 1) * side, :chans] = (
                up * logistic * (1.0 + pre * (1.0 - logistic))
            ).astype(BF16)

    right = g[...].reshape(rows * cells, LANES)
    for a in range(KS):
        left = jnp.concatenate([xst[r + a] for r in range(rows)], axis=1)
        part = jnp.dot(left, right, preferred_element_type=F32)
        for b in range(KS):
            fold = jnp.zeros((GROUP, LANES), F32)
            for k in range(group_count):
                first = b * XROWS + k * GROUP
                fold = jnp.where(group_of == k, part[first : first + GROUP], fold)
            first = (a * KS + b) * GROUP
            gd[first : first + GROUP] = fold
        if a == 0:
            gd[taps * GROUP : taps * GROUP + 8] = part[chans : chans + 8]
            gd[taps * GROUP + 8 :] = jnp.zeros((SUM_LANES - taps * GROUP - 8, LANES), F32)
    turned = gd[...].T
    for i in range(fsdp_count):
        shares[i] = turned[i * share : (i + 1) * share]
    for i in range(fsdp_count // 2):
        keep[i] = shares[fsdp ^ (2 * i)]
        send[i] = shares[fsdp ^ (2 * i + 1)]


def finish_kernel(entries, own, first, second, third, weight_out, bias_out, squares_out):
    del entries
    total = (own[...].astype(F32) + first[...].astype(F32)) + (
        second[...].astype(F32) + third[...].astype(F32)
    )
    count = KS * KS * GROUP
    lane = lax.broadcasted_iota(jnp.int32, total.shape, 1)
    exact = total[:, count : count + 1] + total[:, count + 1 : count + 2]
    total = jnp.where(lane < count, total, jnp.where(lane == count, exact, 0.0))
    squares_out[...] = jnp.full((8, 128), jnp.sum(total * total), F32)
    share = total.shape[0]
    padded = jnp.concatenate([total, jnp.zeros((128 - share, total.shape[1]), F32)], axis=0)
    turned = padded.T
    weight_out[...] = turned[:count, :share].reshape(weight_out.shape)
    bias_out[...] = turned[count : count + 1, :share]


def per_device(fields, weight, bias, cotangent, neighbours):
    tiles, rows, side, chans = fields.shape
    fsdp_count = lax.axis_size("fsdp")
    space_count = lax.axis_size("space")
    fsdp = lax.axis_index("fsdp")
    space = lax.axis_index("space")
    share = chans // fsdp_count
    taps = KS * KS
    tall = rows + 2 * RIM

    flat = weight.reshape(taps * GROUP, share)
    low = flat[: HALF_TAPS * GROUP]
    high = jnp.concatenate([flat[HALF_TAPS * GROUP :], bias[None, :]], axis=0)
    low = jnp.pad(low, ((0, PIECE_ROWS - low.shape[0]), (0, HALF - share)))
    high = jnp.pad(high, ((0, PIECE_ROWS - high.shape[0]), (0, HALF - share)))
    packed = jnp.concatenate([low, high], axis=1)

    even = fsdp % 2 == 0
    first_rows, last_rows = fields[:, :RIM], fields[:, rows - RIM :]

    def outward(i):
        return (i + 1) % fsdp_count if i % 2 else (i - 1) % fsdp_count

    from_outward = swapped(jnp.where(even, first_rows, last_rows), "fsdp", outward)
    from_core = swapped(jnp.where(even, last_rows, first_rows), "fsdp", lambda i: i ^ 1)
    above = jnp.where(even, from_outward, from_core)
    below = jnp.where(even, from_core, from_outward)
    if fsdp_count == 4:
        packed_out = swapped(packed, "fsdp", outward)
        pieces = [
            packed,
            packed_out,
            swapped(packed, "fsdp", lambda i: i ^ 1),
            swapped(packed_out, "fsdp", lambda i: i ^ 1),
        ]
    else:
        gathered = lax.all_gather(packed, "fsdp")
        pieces = [gathered[i] for i in range(fsdp_count)]

    tall_rows = jnp.concatenate([above, fields, below], 1)
    west, east = tall_rows[:, :, :RIM], tall_rows[:, :, side - RIM :]
    far_odd = (space // 2) % 2 == 1
    close_odd = space % 2 == 1
    far0 = hop_pairs(jnp.where(far_odd, west, east), 2, 0)
    far1 = hop_pairs(jnp.where(far_odd, east, west), 2, 1)
    east_far = jnp.where(far_odd, far0, far1)[tiles - 1, :RIM]
    west_far = jnp.where(far_odd, far1, far0)[0, rows + RIM :]
    flat_side = (tiles * tall, RIM, chans)
    to_east = jnp.concatenate([east.reshape(flat_side), east_far], 0)
    to_west = jnp.concatenate([west.reshape(flat_side), west_far], 0)
    close0 = hop_pairs(jnp.where(close_odd, to_west, to_east), 1, 0)
    close1 = hop_pairs(jnp.where(close_odd, to_east, to_west), 1, 1)
    edge0 = hop_pairs(jnp.where(close_odd, below[0], above[tiles - 1]), 1, 0)
    edge1 = hop_pairs(jnp.where(close_odd, above[tiles - 1], below[0]), 1, 1)

    cells = tiles * side
    part = jax.ShapeDtypeStruct((fsdp_count // 2, share, SUM_LANES), F32)
    activations, keep, send = pl.pallas_call(
        functools.partial(main_kernel, len(pieces)),
        out_shape=(jax.ShapeDtypeStruct(fields.shape, BF16), part, part),
        in_specs=[SMEM] + [VMEM] * (10 + len(pieces)),
        out_specs=(VMEM, VMEM, VMEM),
        scratch_shapes=[
            pltpu.VMEM((4 * tiles + 1, tall, RIM, LANES), F32),
            pltpu.VMEM((4 * tiles + 1, tall, RIM, LANES), F32),
            pltpu.VMEM((tall, tiles, side + 16, LANES), F32),
            pltpu.VMEM((tall, cells, KS * LANES), BF16),
            pltpu.VMEM((tall, KS * XROWS, cells), BF16),
            pltpu.VMEM((2 * HALF_TAPS * GROUP, LANES), F32),
            pltpu.VMEM((taps * LANES, LANES), BF16),
            pltpu.VMEM((rows, cells, LANES), BF16),
            pltpu.VMEM((SUM_LANES, LANES), F32),
            pltpu.VMEM((fsdp_count, share, SUM_LANES), F32),
        ],
        compiler_params=pltpu.CompilerParams(vmem_limit_bytes=52 * 1024 * 1024),
        name="section",
    )(
        neighbours, fields, cotangent, above, below,
        far0, far1, close0, close1, edge0, edge1, *pieces,
    )

    held = keep + swapped(send, "fsdp", lambda i: i ^ 1)
    distance = 2
    while held.shape[0] > 1:
        pairs = held.reshape(held.shape[0] // 2, 2, share, SUM_LANES)
        held = pairs[:, 0] + swapped(pairs[:, 1], "fsdp", lambda i: i ^ distance)
        distance *= 2
    held = held[0]
    distance = 1
    while distance * 4 < space_count:
        held = held + swapped(held, "space", lambda i: i ^ distance)
        distance *= 2
    count = taps * GROUP
    lane = lax.broadcasted_iota(jnp.int32, held.shape, 1)
    bias_sum = held[:, count : count + 1]
    bias_low = bias_sum - lax.reduce_precision(bias_sum, 8, 7)
    rounded = jnp.where(lane == count + 1, bias_low, held).astype(BF16)
    others = [swapped(rounded, "space", lambda i, k=k: i ^ (distance * k)) for k in (1, 2, 3)]
    entries = count * chans + chans
    weight_sum, bias_sum, squares = pl.pallas_call(
        functools.partial(finish_kernel, entries),
        out_shape=(
            jax.ShapeDtypeStruct((KS, KS, GROUP, share), F32),
            jax.ShapeDtypeStruct((1, share), F32),
            jax.ShapeDtypeStruct((8, 128), F32),
        ),
        in_specs=[VMEM] * 4,
        out_specs=(VMEM, VMEM, VMEM),
        name="finish",
    )(rounded, *others)
    distance = 1
    while distance < fsdp_count:
        squares = squares + swapped(squares, "fsdp", lambda i: i ^ distance)
        distance *= 2
    scaling = lax.rsqrt(squares[0, 0] / entries + 1e-06)
    return (activations, weight_sum * scaling, bias_sum[0] * scaling)


def solution(mesh):
    return jax.shard_map(
        per_device,
        mesh=mesh,
        in_specs=(
            P("space", "fsdp", None, None),
            P(None, None, None, "fsdp"),
            P("fsdp"),
            P("space", "fsdp", None, None),
            P("space", None),
        ),
        out_specs=(P("space", "fsdp", None, None), P(None, None, None, "fsdp"), P("fsdp")),
        check_vma=False,
    )
```

```python
import functools

import jax
import jax.numpy as jnp
from jax import lax
from jax.experimental import pallas as pl
from jax.experimental.pallas import tpu as pltpu
from jax.sharding import PartitionSpec as P

GROUP = 40
KS = 5
RIM = 2
LANES = 256
HALF = 64
HALF_TAPS = 13
PIECE_ROWS = 528
SUM_LANES = 1024
HALF_SUM = SUM_LANES // 2
BIAS_AT = KS * KS * GROUP - HALF_SUM
XROWS = 208
VMEM = pl.BlockSpec(memory_space=pltpu.VMEM)
SMEM = pl.BlockSpec(memory_space=pltpu.SMEM)
F32 = jnp.float32
BF16 = jnp.bfloat16


def swapped(value, axis, partner):
    count = lax.axis_size(axis)
    pairs = [(i, partner(i)) for i in range(count)]
    return lax.ppermute(value, axis, [p for p in pairs if 0 <= p[1] < count])


def hop_pairs(value, distance, parity):
    def partner(i):
        return i + distance if (i // distance) % 2 == parity else i - distance

    return swapped(value, "space", partner)


def main_kernel(
    piece_count, near, fields, cot, above, below, far0, far1, close0, close1, *rest
):
    pieces = rest[:piece_count]
    act, keep, send = rest[piece_count : piece_count + 3]
    pool_l, pool_r, edges, xf, xs, xst, wc, wd, g, gd, shares = rest[piece_count + 3 :]
    tiles, rows, side, chans = fields.shape
    tall = rows + 2 * RIM
    cells = tiles * side
    fsdp_count = lax.axis_size("fsdp")
    fsdp = lax.axis_index("fsdp")
    space = lax.axis_index("space")
    far_odd = lax.rem(lax.div(space, 2), 2) == 1
    close_odd = lax.rem(space, 2) == 1
    share = chans // fsdp_count

    zero_side = jnp.zeros((tall, RIM, LANES), F32)
    zero_slot = 4 * tiles
    pool_l[zero_slot] = zero_side
    pool_r[zero_slot] = zero_side
    for t in range(tiles):
        lo, hi = far0[t].astype(F32), far1[t].astype(F32)
        pool_l[tiles + t, :, :, :chans] = jnp.where(far_odd, lo, hi)
        pool_r[2 * tiles + t, :, :, :chans] = jnp.where(far_odd, hi, lo)
        lo = close0[t * tall : (t + 1) * tall].astype(F32)
        hi = close1[t * tall : (t + 1) * tall].astype(F32)
        pool_l[2 * tiles + t, :, :, :chans] = jnp.where(close_odd, lo, hi)
        pool_r[tiles + t, :, :, :chans] = jnp.where(close_odd, hi, lo)
    lo = close0[tiles * tall : tiles * tall + RIM].astype(F32)
    hi = close1[tiles * tall : tiles * tall + RIM].astype(F32)
    pool_l[tiles - 1, :RIM, :, :chans] = jnp.where(close_odd, lo, hi)
    pool_r[3 * tiles, rows + RIM :, :, :chans] = jnp.where(close_odd, hi, lo)
    lo = close0[tiles * tall + RIM :].astype(F32)
    hi = close1[tiles * tall + RIM :].astype(F32)
    edges[0, :, :, :chans] = jnp.where(close_odd, lo, hi)
    edges[1, :, :, :chans] = jnp.where(close_odd, hi, lo)
    edge_north = jnp.stack([edges[0, :, r, :chans] for r in range(RIM)])
    edge_south = jnp.stack([edges[1, :, r, :chans] for r in range(RIM)])

    lane = lax.broadcasted_iota(jnp.int32, (tiles, side + 16, 128), 2)
    one_behind = jnp.where(lane == chans - 128, 1.0, 0.0).astype(F32)
    for r in range(tall):
        xf[r, :, :, 128:] = one_behind
    for t in range(tiles):
        top, bottom = above[t].astype(F32), below[t].astype(F32)
        centre = fields[t].astype(F32)
        for part, first in ((top, 0), (centre, RIM), (bottom, RIM + rows)):
            length = part.shape[0]
            pool_l[3 * tiles + t, first : first + length, :, :chans] = part[:, side - RIM :]
            pool_r[t, first : first + length, :, :chans] = part[:, :RIM]
        xf[RIM : RIM + rows, t, 8 : 8 + side, :chans] = centre
        north = edge_north if t == 0 else above[t - 1].astype(F32)
        south = edge_south if t == tiles - 1 else below[t + 1].astype(F32)
        north = jnp.where(near[t, 0] >= 0, north, 0.0)
        south = jnp.where(near[t, 1] >= 0, south, 0.0)
        xf[:RIM, t, 8 : 8 + side, :chans] = jnp.where(fsdp == 0, north, top)
        xf[RIM + rows :, t, 8 : 8 + side, :chans] = jnp.where(fsdp == fsdp_count - 1, south, bottom)

    def slot(tile_id, first):
        return jnp.where(tile_id < 0, zero_slot, jnp.clip(tile_id - first * tiles, 0, zero_slot))

    for t in range(tiles):
        for pool, column, first, beside, up, down in (
            (pool_l, 6, space - 3, near[t, 2], near[t, 4], near[t, 6]),
            (pool_r, 8 + side, space, near[t, 3], near[t, 5], near[t, 7]),
        ):
            mid = slot(beside, first)
            top = jnp.where(fsdp == 0, slot(up, first), mid)
            bottom = jnp.where(fsdp == fsdp_count - 1, slot(down, first), mid)
            into = pl.ds(column, RIM)
            xf[RIM : RIM + rows, t, into, :chans] = pool[mid, RIM : RIM + rows, :, :chans]
            xf[:RIM, t, into, :chans] = pool[top, :RIM, :, :chans]
            xf[RIM + rows :, t, into, :chans] = pool[bottom, RIM + rows :, :, :chans]

    lined = jnp.concatenate([p[...] for p in pieces], axis=1)
    owner = []
    for i in range(piece_count):
        if piece_count == fsdp_count and fsdp_count != 4:
            owner.append(i)
        else:
            owner.append((fsdp, 3 - fsdp, fsdp ^ 1, fsdp ^ 2)[i])
    from_lane = lax.broadcasted_iota(jnp.int32, (128, LANES), 0)
    to_lane = lax.broadcasted_iota(jnp.int32, (128, LANES), 1)
    for half in range(2):
        picks = []
        for i in range(piece_count):
            inside = from_lane - half * HALF
            valid = (inside >= 0) & (inside < share) & (to_lane == owner[i] * share + inside)
            picks.append(jnp.where(valid, 1.0, 0.0).astype(BF16))
        full = jnp.dot(lined, jnp.concatenate(picks, axis=0), preferred_element_type=F32)
        wc[half * HALF_TAPS * GROUP : (half + 1) * HALF_TAPS * GROUP, :] = full[: HALF_TAPS * GROUP]
    group_count = chans // GROUP
    group_of = lax.broadcasted_iota(jnp.int32, (GROUP, LANES), 1) // GROUP
    taps = KS * KS
    for tap in range(taps):
        one = wc[tap * GROUP : (tap + 1) * GROUP]
        blocks = [jnp.where(group_of == k, one, 0.0) for k in range(group_count)]
        if tap == taps // 2:
            blocks.append(wc[taps * GROUP : taps * GROUP + 8])
        else:
            blocks.append(jnp.zeros((8, LANES), F32))
        blocks.append(jnp.zeros((LANES - chans - 8, LANES), F32))
        wd[tap * LANES : (tap + 1) * LANES] = jnp.concatenate(blocks, axis=0).astype(BF16)

    @pl.loop(0, tall)
    def _(r):
        for b in range(KS):
            piece = xf[r, :, 6 + b : 6 + b + side, :].astype(BF16).reshape(cells, LANES)
            xs[r, :, b * LANES : (b + 1) * LANES] = piece
            xst[r, b * XROWS : (b + 1) * XROWS, :] = piece.T[:XROWS]

    step = min(8, rows)
    for r0 in range(0, rows, step):
        total = None
        for a in range(KS):
            left = xs[r0 + a : r0 + a + step].reshape(step * cells, KS * LANES)
            right = wd[a * KS * LANES : (a + 1) * KS * LANES]
            part = jnp.dot(left, right, preferred_element_type=F32)
            total = part if total is None else total + part
        total = total.reshape(step, tiles, side, LANES)
        for t in range(tiles):
            pre = total[:, t, :, :chans]
            logistic = 1.0 / (1.0 + jnp.exp(-pre))
            act[t, r0 : r0 + step] = (pre * logistic).astype(BF16)
            up = cot[t, r0 : r0 + step].astype(F32)
            g[r0 : r0 + step, t * side : (t + 1) * side, :chans] = (
                up * logistic * (1.0 + pre * (1.0 - logistic))
            ).astype(BF16)

    right = g[...].reshape(rows * cells, LANES)
    for a in range(KS):
        left = jnp.concatenate([xst[r + a] for r in range(rows)], axis=1)
        part = jnp.dot(left, right, preferred_element_type=F32)
        for b in range(KS):
            fold = jnp.zeros((GROUP, LANES), F32)
            for k in range(group_count):
                first = b * XROWS + k * GROUP
                fold = jnp.where(group_of == k, part[first : first + GROUP], fold)
            first = (a * KS + b) * GROUP
            gd[first : first + GROUP] = fold
        if a == 0:
            gd[taps * GROUP : taps * GROUP + 8] = part[chans : chans + 8]
            gd[taps * GROUP + 8 :] = jnp.zeros((SUM_LANES - taps * GROUP - 8, LANES), F32)
    turned = gd[...].T
    for i in range(fsdp_count):
        shares[i] = turned[i * share : (i + 1) * share]
    for i in range(fsdp_count // 2):
        for into, whose in ((keep, fsdp ^ (2 * i)), (send, fsdp ^ (2 * i + 1))):
            low, high = shares[whose, :, :HALF_SUM], shares[whose, :, HALF_SUM:]
            into[i, 0] = jnp.where(close_odd, high, low)
            into[i, 1] = jnp.where(close_odd, low, high)


def bias_lane(shape, half, at):
    lane = lax.broadcasted_iota(jnp.int32, shape, len(shape) - 1)
    return (lane == at) & (half == 1)


def narrowed(value, half):
    lead = value.shape[:-2]
    index = lax.broadcasted_iota(jnp.int32, value.shape, len(lead) - 1)
    whose = index ^ half
    bias_sum = value[..., BIAS_AT : BIAS_AT + 1] + value[..., BIAS_AT + 1 : BIAS_AT + 2]
    bias_low = bias_sum - lax.reduce_precision(bias_sum, 8, 7)
    value = jnp.where(bias_lane(value.shape, whose, BIAS_AT), bias_sum, value)
    return jnp.where(bias_lane(value.shape, whose, BIAS_AT + 1), bias_low, value).astype(BF16)


def scale_kernel(entries, own, beside, *rest):
    squares, (weight_out, bias_out) = rest[:-2], rest[-2:]
    odd = lax.rem(lax.axis_index("space"), 2) == 1
    count = KS * KS * GROUP
    share = own.shape[0]
    sums = [value[0:1, :] for value in squares]
    while len(sums) > 1:
        sums = [a + b for a, b in zip(sums[::2], sums[1::2])]
    scaling = lax.rsqrt(jnp.sum(sums[0], axis=1, keepdims=True) / entries + 1e-06)
    low = jnp.where(odd, beside[...], own[...])
    high = jnp.where(odd, own[...], beside[...])
    whole = jnp.concatenate([low, high], axis=1) * scaling
    whole = jnp.concatenate([whole, jnp.zeros((128 - share, SUM_LANES), F32)], axis=0)
    turned = whole.T
    weight_out[...] = turned[:count, :share].reshape(weight_out.shape)
    bias_out[...] = turned[count : count + 1, :share]


def pack_kernel(fields, weight, bias, rows_outward, rows_core, packed, west, east, wide):
    tiles, rows, side, chans = fields.shape
    share = weight.shape[2]
    even = lax.rem(lax.axis_index("fsdp"), 2) == 0

    @pl.when(even)
    def _():
        rows_outward[...] = fields[:, :RIM]
        rows_core[...] = fields[:, rows - RIM :]

    @pl.when(jnp.logical_not(even))
    def _():
        rows_core[...] = fields[:, :RIM]
        rows_outward[...] = fields[:, rows - RIM :]

    west[...] = fields[:, :, :RIM]
    east[...] = fields[:, :, side - RIM :]
    high = KS * KS - HALF_TAPS
    wide[...] = jnp.zeros(wide.shape, F32)
    wide[: HALF_TAPS * GROUP, :share] = weight[:HALF_TAPS].astype(F32).reshape(-1, share)
    wide[: high * GROUP, HALF : HALF + share] = weight[HALF_TAPS:].astype(F32).reshape(-1, share)
    wide[high * GROUP : high * GROUP + 1, HALF : HALF + share] = bias[...].astype(F32)
    packed[...] = wide[...].astype(BF16)


def per_device(fields, weight, bias, cotangent, neighbours):
    tiles, rows, side, chans = fields.shape
    fsdp_count = lax.axis_size("fsdp")
    space_count = lax.axis_size("space")
    fsdp = lax.axis_index("fsdp")
    space = lax.axis_index("space")
    share = chans // fsdp_count
    taps = KS * KS
    tall = rows + 2 * RIM

    even = fsdp % 2 == 0
    first_rows, last_rows = fields[:, :RIM], fields[:, rows - RIM :]

    def outward(i):
        return (i + 1) % fsdp_count if i % 2 else (i - 1) % fsdp_count

    def joined(name_outward, name_core):
        up = jnp.where(even, name_outward, name_core)
        return up, jnp.where(even, name_core, name_outward)

    def inward(i):
        return i ^ 1

    first_ends = jnp.concatenate([first_rows[:, :, :RIM], first_rows[:, :, side - RIM :]], 2)
    last_ends = jnp.concatenate([last_rows[:, :, :RIM], last_rows[:, :, side - RIM :]], 2)
    ends_outward = swapped(jnp.where(even, first_ends, last_ends), "fsdp", outward)
    ends_core = swapped(jnp.where(even, last_ends, first_ends), "fsdp", inward)
    rim = jax.ShapeDtypeStruct((tiles, RIM, side, chans), BF16)
    columns = jax.ShapeDtypeStruct((tiles, rows, RIM, chans), BF16)
    rows_outward, rows_core, packed, west_own, east_own = pl.pallas_call(
        pack_kernel,
        out_shape=(rim, rim, jax.ShapeDtypeStruct((PIECE_ROWS, 128), BF16), columns, columns),
        in_specs=[VMEM] * 3,
        out_specs=(VMEM,) * 5,
        scratch_shapes=[pltpu.VMEM((PIECE_ROWS, 128), F32)],
        name="pack",
    )(fields, weight.reshape(taps, GROUP, share), bias[None, :])
    from_outward = swapped(rows_outward, "fsdp", outward)
    from_core = swapped(rows_core, "fsdp", inward)
    if fsdp_count == 4:
        packed_out = swapped(packed, "fsdp", outward)
        packed_core = swapped(packed, "fsdp", inward)
    ends_above, ends_below = joined(ends_outward, ends_core)

    west = jnp.concatenate([ends_above[:, :, :RIM], west_own, ends_below[:, :, :RIM]], 1)
    east = jnp.concatenate([ends_above[:, :, RIM:], east_own, ends_below[:, :, RIM:]], 1)
    far_odd = (space // 2) % 2 == 1
    close_odd = space % 2 == 1
    far0 = hop_pairs(jnp.where(far_odd, west, east), 2, 0)
    far1 = hop_pairs(jnp.where(far_odd, east, west), 2, 1)
    if fsdp_count == 4:
        far0, packed_out = lax.optimization_barrier((far0, packed_out))
        packed_last = swapped(packed_out, "fsdp", inward)
    above, below = joined(from_outward, from_core)
    east_far = jnp.where(far_odd, far0, far1)[tiles - 1, :RIM]
    west_far = jnp.where(far_odd, far1, far0)[0, rows + RIM :]
    flat_side = (tiles * tall, RIM, chans)
    edge_east = jnp.swapaxes(above[tiles - 1], 0, 1)
    edge_west = jnp.swapaxes(below[0], 0, 1)
    to_east = jnp.concatenate([east.reshape(flat_side), east_far, edge_east], 0)
    to_west = jnp.concatenate([west.reshape(flat_side), west_far, edge_west], 0)
    close0 = hop_pairs(jnp.where(close_odd, to_west, to_east), 1, 0)
    close1 = hop_pairs(jnp.where(close_odd, to_east, to_west), 1, 1)
    if fsdp_count == 4:
        pieces = [packed, packed_out, packed_core, packed_last]
    else:
        gathered = lax.all_gather(packed, "fsdp")
        pieces = [gathered[i] for i in range(fsdp_count)]

    cells = tiles * side
    part = jax.ShapeDtypeStruct((fsdp_count // 2, 2, share, HALF_SUM), F32)
    activations, keep, send = pl.pallas_call(
        functools.partial(main_kernel, len(pieces)),
        out_shape=(jax.ShapeDtypeStruct(fields.shape, BF16), part, part),
        in_specs=[SMEM] + [VMEM] * (8 + len(pieces)),
        out_specs=(VMEM, VMEM, VMEM),
        scratch_shapes=[
            pltpu.VMEM((4 * tiles + 1, tall, RIM, LANES), F32),
            pltpu.VMEM((4 * tiles + 1, tall, RIM, LANES), F32),
            pltpu.VMEM((2, side, RIM, LANES), F32),
            pltpu.VMEM((tall, tiles, side + 16, LANES), F32),
            pltpu.VMEM((tall, cells, KS * LANES), BF16),
            pltpu.VMEM((tall, KS * XROWS, cells), BF16),
            pltpu.VMEM((2 * HALF_TAPS * GROUP, LANES), F32),
            pltpu.VMEM((taps * LANES, LANES), BF16),
            pltpu.VMEM((rows, cells, LANES), BF16),
            pltpu.VMEM((SUM_LANES, LANES), F32),
            pltpu.VMEM((fsdp_count, share, SUM_LANES), F32),
        ],
        compiler_params=pltpu.CompilerParams(vmem_limit_bytes=52 * 1024 * 1024),
        name="section",
    )(
        neighbours, fields, cotangent, above, below,
        far0, far1, close0, close1, *pieces,
    )

    held = keep + swapped(send, "fsdp", lambda i: i ^ 1)
    half = space % 2
    distance = 2
    while held.shape[0] > 1:
        pairs = held.reshape(held.shape[0] // 2, 2, 2, share, HALF_SUM)
        sent = narrowed(pairs[:, 1], half)
        held = pairs[:, 0] + swapped(sent, "fsdp", lambda i: i ^ distance).astype(F32)
        distance *= 2
    held = held[0, 0] + swapped(held[0, 1], "space", lambda i: i ^ 1)
    distance = 2
    while distance * 4 < space_count:
        held = held + swapped(held, "space", lambda i: i ^ distance)
        distance *= 2
    rounded = narrowed(jnp.stack([held]), half)[0]
    others = [swapped(rounded, "space", lambda i, k=k: i ^ (distance * k)) for k in (1, 2, 3)]
    total = (rounded.astype(F32) + others[0].astype(F32)) + (
        others[1].astype(F32) + others[2].astype(F32)
    )
    exact = total[:, BIAS_AT : BIAS_AT + 1] + total[:, BIAS_AT + 1 : BIAS_AT + 2]
    total = jnp.where(bias_lane(total.shape, half, BIAS_AT), exact, total)
    total = jnp.where(bias_lane(total.shape, half, BIAS_AT + 1), 0.0, total)
    total_beside = swapped(total, "space", lambda i: i ^ 1)

    squares = jnp.sum(total * total, 0, keepdims=True) + jnp.sum(total_beside * total_beside, 0, keepdims=True)
    squares = jnp.broadcast_to(squares, (8, HALF_SUM))
    all_squares = [squares] + [
        swapped(squares, "fsdp", lambda i, k=k: i ^ k) for k in range(1, fsdp_count)
    ]
    weight_step, bias_step = pl.pallas_call(
        functools.partial(scale_kernel, taps * GROUP * chans + chans),
        out_shape=(
            jax.ShapeDtypeStruct((KS, KS, GROUP, share), F32),
            jax.ShapeDtypeStruct((1, share), F32),
        ),
        in_specs=[VMEM] * (2 + fsdp_count),
        out_specs=(VMEM, VMEM),
        name="scale",
    )(total, total_beside, *all_squares)
    return (activations, weight_step, bias_step[0])


def solution(mesh):
    return jax.shard_map(
        per_device,
        mesh=mesh,
        in_specs=(
            P("space", "fsdp", None, None),
            P(None, None, None, "fsdp"),
            P("fsdp"),
            P("space", "fsdp", None, None),
            P("space", None),
        ),
        out_specs=(P("space", "fsdp", None, None), P(None, None, None, "fsdp"), P("fsdp")),
        check_vma=False,
    )
```

```python
import functools

import jax
import jax.numpy as jnp
from jax import lax
from jax.experimental import pallas as pl
from jax.experimental.pallas import tpu as pltpu
from jax.sharding import PartitionSpec as P

GROUP = 40
KS = 5
RIM = 2
LANES = 256
HALF = 64
HALF_TAPS = 13
PIECE_ROWS = 528
SUM_LANES = 1024
STEP = 4
HALF_SUM = SUM_LANES // 2
BIAS_AT = KS * KS * GROUP - HALF_SUM
XROWS = 208
VMEM = pl.BlockSpec(memory_space=pltpu.VMEM)
ANY = pl.BlockSpec(memory_space=pl.ANY)
SMEM = pl.BlockSpec(memory_space=pltpu.SMEM)
F32 = jnp.float32
SMALL = pltpu.CompilerParams(vmem_limit_bytes=12 * 1024 * 1024)
BF16 = jnp.bfloat16


def swapped(value, axis, partner):
    count = lax.axis_size(axis)
    pairs = [(i, partner(i)) for i in range(count)]
    return lax.ppermute(value, axis, [p for p in pairs if 0 <= p[1] < count])


def hop_pairs(value, distance, parity):
    def partner(i):
        return i + distance if (i // distance) % 2 == parity else i - distance

    return swapped(value, "space", partner)


def main_kernel(
    piece_count, near, fields_far, cot_far, above, below, far0, far1, close0, close1, edge, *rest
):
    pieces = rest[:piece_count]
    act_far, keep, send = rest[piece_count : piece_count + 3]
    fields, cot, act, sems, pool_l, pool_r, xf, xs, xst, wc, wd, g, gd, shares = rest[piece_count + 3 :]
    fields_in = pltpu.make_async_copy(fields_far, fields, sems.at[0])
    cot_in = pltpu.make_async_copy(cot_far, cot, sems.at[1])
    fields_in.start()
    cot_in.start()
    tiles, rows, side, chans = fields.shape
    tall = rows + 2 * RIM
    cells = tiles * side
    fsdp_count = lax.axis_size("fsdp")
    fsdp = lax.axis_index("fsdp")
    space = lax.axis_index("space")
    far_odd = lax.rem(lax.div(space, 2), 2) == 1
    close_odd = lax.rem(space, 2) == 1
    share = chans // fsdp_count

    lined = jnp.concatenate([p[...] for p in pieces], axis=1)
    owner = []
    for i in range(piece_count):
        if piece_count == fsdp_count and fsdp_count != 4:
            owner.append(i)
        else:
            owner.append((fsdp, 3 - fsdp, fsdp ^ 1, fsdp ^ 2)[i])
    from_lane = lax.broadcasted_iota(jnp.int32, (128, LANES), 0)
    to_lane = lax.broadcasted_iota(jnp.int32, (128, LANES), 1)
    for half in range(2):
        picks = []
        for i in range(piece_count):
            inside = from_lane - half * HALF
            valid = (inside >= 0) & (inside < share) & (to_lane == owner[i] * share + inside)
            picks.append(jnp.where(valid, 1.0, 0.0).astype(BF16))
        full = jnp.dot(lined, jnp.concatenate(picks, axis=0), preferred_element_type=F32)
        wc[half * HALF_TAPS * GROUP : (half + 1) * HALF_TAPS * GROUP, :] = full[: HALF_TAPS * GROUP]
    group_count = chans // GROUP
    group_of = lax.broadcasted_iota(jnp.int32, (GROUP, LANES), 1) // GROUP
    taps = KS * KS
    for tap in range(taps):
        one = wc[tap * GROUP : (tap + 1) * GROUP]
        blocks = [jnp.where(group_of == k, one, 0.0) for k in range(group_count)]
        if tap == taps // 2:
            blocks.append(wc[taps * GROUP : taps * GROUP + 8])
        else:
            blocks.append(jnp.zeros((8, LANES), F32))
        blocks.append(jnp.zeros((LANES - chans - 8, LANES), F32))
        wd[tap * LANES : (tap + 1) * LANES] = jnp.concatenate(blocks, axis=0).astype(BF16)

    zero_side = jnp.zeros((tall, RIM, LANES), F32)
    zero_slot = 4 * tiles
    pool_l[zero_slot] = zero_side
    pool_r[zero_slot] = zero_side
    for t in range(tiles):
        lo, hi = far0[t].astype(F32), far1[t].astype(F32)
        pool_l[tiles + t, :, :, :chans] = jnp.where(far_odd, lo, hi)
        pool_r[2 * tiles + t, :, :, :chans] = jnp.where(far_odd, hi, lo)
        lo = close0[t * tall : (t + 1) * tall].astype(F32)
        hi = close1[t * tall : (t + 1) * tall].astype(F32)
        pool_l[2 * tiles + t, :, :, :chans] = jnp.where(close_odd, lo, hi)
        pool_r[tiles + t, :, :, :chans] = jnp.where(close_odd, hi, lo)
    lo = close0[tiles * tall :].astype(F32)
    hi = close1[tiles * tall :].astype(F32)
    pool_l[tiles - 1, :RIM, :, :chans] = jnp.where(close_odd, lo, hi)
    pool_r[3 * tiles, rows + RIM :, :, :chans] = jnp.where(close_odd, hi, lo)

    fields_in.wait()

    lane = lax.broadcasted_iota(jnp.int32, (tiles, side + 16, 128), 2)
    one_behind = jnp.where(lane == chans - 128, 1.0, 0.0).astype(F32)
    for r in range(tall):
        xf[r, :, :, 128:] = one_behind
    for t in range(tiles):
        top, bottom = above[t].astype(F32), below[t].astype(F32)
        centre = fields[t].astype(F32)
        for part, first in ((top, 0), (centre, RIM), (bottom, RIM + rows)):
            length = part.shape[0]
            pool_l[3 * tiles + t, first : first + length, :, :chans] = part[:, side - RIM :]
            pool_r[t, first : first + length, :, :chans] = part[:, :RIM]
        xf[RIM : RIM + rows, t, 8 : 8 + side, :chans] = centre
        north = edge[...].astype(F32) if t == 0 else above[t - 1].astype(F32)
        south = edge[...].astype(F32) if t == tiles - 1 else below[t + 1].astype(F32)
        north = jnp.where(near[t, 0] >= 0, north, 0.0)
        south = jnp.where(near[t, 1] >= 0, south, 0.0)
        xf[:RIM, t, 8 : 8 + side, :chans] = jnp.where(fsdp == 0, north, top)
        xf[RIM + rows :, t, 8 : 8 + side, :chans] = jnp.where(fsdp == fsdp_count - 1, south, bottom)

    def slot(tile_id, first):
        return jnp.where(tile_id < 0, zero_slot, jnp.clip(tile_id - first * tiles, 0, zero_slot))

    for t in range(tiles):
        for pool, column, first, beside, up, down in (
            (pool_l, 6, space - 3, near[t, 2], near[t, 4], near[t, 6]),
            (pool_r, 8 + side, space, near[t, 3], near[t, 5], near[t, 7]),
        ):
            mid = slot(beside, first)
            top = jnp.where(fsdp == 0, slot(up, first), mid)
            bottom = jnp.where(fsdp == fsdp_count - 1, slot(down, first), mid)
            into = pl.ds(column, RIM)
            xf[RIM : RIM + rows, t, into, :chans] = pool[mid, RIM : RIM + rows, :, :chans]
            xf[:RIM, t, into, :chans] = pool[top, :RIM, :, :chans]
            xf[RIM + rows :, t, into, :chans] = pool[bottom, RIM + rows :, :, :chans]

    def shift(some_rows):
        for r in some_rows:
            for b in range(KS):
                piece = xf[r, :, 6 + b : 6 + b + side, :].astype(BF16).reshape(cells, LANES)
                xs[r, :, b * LANES : (b + 1) * LANES] = piece
                xst[r, b * XROWS : (b + 1) * XROWS, :] = piece.T[:XROWS]

    cot_in.wait()
    act_out = []
    step = min(STEP, rows)
    reach = step + KS - 1
    shift(range(reach))
    for r0 in range(0, rows, step):
        if r0 + step < rows:
            shift(range(r0 + reach, r0 + reach + step))
        total = None
        for a in range(KS):
            left = xs[r0 + a : r0 + a + step].reshape(step * cells, KS * LANES)
            right = wd[a * KS * LANES : (a + 1) * KS * LANES]
            part = jnp.dot(left, right, preferred_element_type=F32)
            total = part if total is None else total + part
        total = total.reshape(step, tiles, side, LANES)
        for t in range(tiles):
            pre = total[:, t, :, :chans]
            logistic = 1.0 / (1.0 + jnp.exp(-pre))
            act[t, r0 : r0 + step] = (pre * logistic).astype(BF16)
            up = cot[t, r0 : r0 + step].astype(F32)
            g[r0 : r0 + step, t * side : (t + 1) * side, :chans] = (
                up * logistic * (1.0 + pre * (1.0 - logistic))
            ).astype(BF16)

        chunk = pl.ds(r0, step)
        act_out.append(
            pltpu.make_async_copy(act.at[:, chunk], act_far.at[:, chunk], sems.at[2 + r0 // step])
        )
        act_out[-1].start()

    right = g[...].reshape(rows * cells, LANES)
    for a in range(KS):
        left = jnp.concatenate([xst[r + a] for r in range(rows)], axis=1)
        part = jnp.dot(left, right, preferred_element_type=F32)
        for b in range(KS):
            fold = jnp.zeros((GROUP, LANES), F32)
            for k in range(group_count):
                first = b * XROWS + k * GROUP
                fold = jnp.where(group_of == k, part[first : first + GROUP], fold)
            first = (a * KS + b) * GROUP
            gd[first : first + GROUP] = fold
        if a == 0:
            gd[taps * GROUP : taps * GROUP + 8] = part[chans : chans + 8]
            gd[taps * GROUP + 8 :] = jnp.zeros((SUM_LANES - taps * GROUP - 8, LANES), F32)
    turned = gd[...].T
    for i in range(fsdp_count):
        shares[i] = turned[i * share : (i + 1) * share]
    for i in range(fsdp_count // 2):
        for into, whose in ((keep, fsdp ^ (2 * i)), (send, fsdp ^ (2 * i + 1))):
            low, high = shares[whose, :, :HALF_SUM], shares[whose, :, HALF_SUM:]
            into[i, 0] = jnp.where(close_odd, high, low)
            into[i, 1] = jnp.where(close_odd, low, high)
    for copy in act_out:
        copy.wait()


def bias_lane(shape, half, at):
    lane = lax.broadcasted_iota(jnp.int32, shape, len(shape) - 1)
    return (lane == at) & (half == 1)


def narrowed(value, half):
    lead = value.shape[:-2]
    index = lax.broadcasted_iota(jnp.int32, value.shape, len(lead) - 1)
    whose = index ^ half
    bias_sum = value[..., BIAS_AT : BIAS_AT + 1] + value[..., BIAS_AT + 1 : BIAS_AT + 2]
    bias_low = bias_sum - lax.reduce_precision(bias_sum, 8, 7)
    value = jnp.where(bias_lane(value.shape, whose, BIAS_AT), bias_sum, value)
    return jnp.where(bias_lane(value.shape, whose, BIAS_AT + 1), bias_low, value).astype(BF16)


def scale_kernel(entries, own, beside, *rest):
    squares, (weight_out, bias_out) = rest[:-2], rest[-2:]
    odd = lax.rem(lax.axis_index("space"), 2) == 1
    count = KS * KS * GROUP
    share = own.shape[0]
    sums = [value[0:1, :] for value in squares]
    while len(sums) > 1:
        sums = [a + b for a, b in zip(sums[::2], sums[1::2])]
    scaling = lax.rsqrt(jnp.sum(sums[0], axis=1, keepdims=True) / entries + 1e-06)
    low = jnp.where(odd, beside[...], own[...])
    high = jnp.where(odd, own[...], beside[...])
    whole = jnp.concatenate([low, high], axis=1) * scaling
    whole = jnp.concatenate([whole, jnp.zeros((128 - share, SUM_LANES), F32)], axis=0)
    turned = whole.T
    weight_out[...] = turned[:count, :share].reshape(weight_out.shape)
    bias_out[...] = turned[count : count + 1, :share]


def rim_kernel(
    fields, ends_outward, ends_core, rows_outward, rows_core, west, east, rims, sides, sems
):
    rows, side = fields.shape[1:3]
    even = lax.rem(lax.axis_index("fsdp"), 2) == 0
    copies = [
        pltpu.make_async_copy(fields.at[:, pl.ds(0, RIM)], rims.at[0], sems.at[0]),
        pltpu.make_async_copy(fields.at[:, pl.ds(rows - RIM, RIM)], rims.at[1], sems.at[1]),
        pltpu.make_async_copy(fields.at[:, :, pl.ds(0, 16)], sides.at[0], sems.at[2]),
        pltpu.make_async_copy(fields.at[:, :, pl.ds(side - 16, 16)], sides.at[1], sems.at[3]),
    ]
    for copy in copies:
        copy.start()
    for copy in copies:
        copy.wait()

    def give(first_ends, first_rows, last_ends, last_rows):
        for i, (ends, outer) in enumerate(((first_ends, first_rows), (last_ends, last_rows))):
            outer[...] = rims[i]
            ends[:, :, :RIM] = rims[i, :, :, :RIM]
            ends[:, :, RIM:] = rims[i, :, :, side - RIM :]

    @pl.when(even)
    def _():
        give(ends_outward, rows_outward, ends_core, rows_core)

    @pl.when(jnp.logical_not(even))
    def _():
        give(ends_core, rows_core, ends_outward, rows_outward)

    west[...] = sides[0, :, :, :RIM]
    east[...] = sides[1, :, :, 16 - RIM :]


def pack_kernel(weight, bias, packed, wide):
    share = weight.shape[2]
    high = KS * KS - HALF_TAPS
    wide[...] = jnp.zeros(wide.shape, F32)
    wide[: HALF_TAPS * GROUP, :share] = weight[:HALF_TAPS].astype(F32).reshape(-1, share)
    wide[: high * GROUP, HALF : HALF + share] = weight[HALF_TAPS:].astype(F32).reshape(-1, share)
    wide[high * GROUP : high * GROUP + 1, HALF : HALF + share] = bias[...].astype(F32)
    packed[...] = wide[...].astype(BF16)


def per_device(fields, weight, bias, cotangent, neighbours):
    tiles, rows, side, chans = fields.shape
    fsdp_count = lax.axis_size("fsdp")
    space_count = lax.axis_size("space")
    fsdp = lax.axis_index("fsdp")
    space = lax.axis_index("space")
    share = chans // fsdp_count
    taps = KS * KS
    tall = rows + 2 * RIM

    even = fsdp % 2 == 0

    def outward(i):
        return (i + 1) % fsdp_count if i % 2 else (i - 1) % fsdp_count

    def joined(name_outward, name_core):
        up = jnp.where(even, name_outward, name_core)
        return up, jnp.where(even, name_core, name_outward)

    def inward(i):
        return i ^ 1

    ends = jax.ShapeDtypeStruct((tiles, RIM, 2 * RIM, chans), BF16)
    rim = jax.ShapeDtypeStruct((tiles, RIM, side, chans), BF16)
    columns = jax.ShapeDtypeStruct((tiles, rows, RIM, chans), BF16)
    ends_outward, ends_core, rows_outward, rows_core, west_own, east_own = pl.pallas_call(
        rim_kernel,
        out_shape=(ends, ends, rim, rim, columns, columns),
        in_specs=[ANY],
        out_specs=(VMEM,) * 6,
        scratch_shapes=[
            pltpu.VMEM((2, tiles, RIM, side, chans), BF16),
            pltpu.VMEM((2, tiles, rows, 16, chans), BF16),
            pltpu.SemaphoreType.DMA((4,)),
        ],
        compiler_params=SMALL,
        name="rims",
    )(fields)
    packed = pl.pallas_call(
        pack_kernel,
        out_shape=jax.ShapeDtypeStruct((PIECE_ROWS, 128), BF16),
        in_specs=[VMEM] * 2,
        out_specs=VMEM,
        scratch_shapes=[pltpu.VMEM((PIECE_ROWS, 128), F32)],
        compiler_params=SMALL,
        name="pack",
    )(weight.reshape(taps, GROUP, share), bias[None, :])
    ends_outward = swapped(ends_outward, "fsdp", outward)
    ends_core = swapped(ends_core, "fsdp", inward)
    from_outward = swapped(rows_outward, "fsdp", outward)
    from_core = swapped(rows_core, "fsdp", inward)
    if fsdp_count == 4:
        packed_out = swapped(packed, "fsdp", outward)
        packed_core = swapped(packed, "fsdp", inward)
    ends_above, ends_below = joined(ends_outward, ends_core)

    west = jnp.concatenate([ends_above[:, :, :RIM], west_own, ends_below[:, :, :RIM]], 1)
    east = jnp.concatenate([ends_above[:, :, RIM:], east_own, ends_below[:, :, RIM:]], 1)
    far_odd = (space // 2) % 2 == 1
    close_odd = space % 2 == 1
    far0 = hop_pairs(jnp.where(far_odd, west, east), 2, 0)
    far1 = hop_pairs(jnp.where(far_odd, east, west), 2, 1)
    if fsdp_count == 4:
        far1, packed_out = lax.optimization_barrier((far1, packed_out))
        packed_last = swapped(packed_out, "fsdp", inward)
    far1, from_outward, from_core = lax.optimization_barrier((far1, from_outward, from_core))
    above, below = joined(from_outward, from_core)
    east_far = jnp.where(far_odd, far0, far1)[tiles - 1, :RIM]
    west_far = jnp.where(far_odd, far1, far0)[0, rows + RIM :]
    flat_side = (tiles * tall, RIM, chans)
    last_row = fsdp_count - 1
    edge_pairs = [(i * fsdp_count, (i + 1) * fsdp_count) for i in range(space_count - 1)]
    edge_pairs += [
        ((i + 1) * fsdp_count + last_row, i * fsdp_count + last_row) for i in range(space_count - 1)
    ]
    edge = lax.ppermute(
        jnp.where(fsdp == 0, above[tiles - 1], below[0]), ("space", "fsdp"), edge_pairs
    )
    to_east = jnp.concatenate([east.reshape(flat_side), east_far], 0)
    to_west = jnp.concatenate([west.reshape(flat_side), west_far], 0)
    close0 = hop_pairs(jnp.where(close_odd, to_west, to_east), 1, 0)
    close1 = hop_pairs(jnp.where(close_odd, to_east, to_west), 1, 1)
    if fsdp_count == 4:
        pieces = [packed, packed_out, packed_core, packed_last]
    else:
        gathered = lax.all_gather(packed, "fsdp")
        pieces = [gathered[i] for i in range(fsdp_count)]

    cells = tiles * side
    part = jax.ShapeDtypeStruct((fsdp_count // 2, 2, share, HALF_SUM), F32)
    activations, keep, send = pl.pallas_call(
        functools.partial(main_kernel, len(pieces)),
        out_shape=(jax.ShapeDtypeStruct(fields.shape, BF16), part, part),
        in_specs=[SMEM, ANY, ANY] + [VMEM] * (7 + len(pieces)),
        out_specs=(ANY, VMEM, VMEM),
        scratch_shapes=[
            pltpu.VMEM(fields.shape, BF16),
            pltpu.VMEM(fields.shape, BF16),
            pltpu.VMEM(fields.shape, BF16),
            pltpu.SemaphoreType.DMA((2 + rows // min(STEP, rows),)),
            pltpu.VMEM((4 * tiles + 1, tall, RIM, LANES), F32),
            pltpu.VMEM((4 * tiles + 1, tall, RIM, LANES), F32),
            pltpu.VMEM((tall, tiles, side + 16, LANES), F32),
            pltpu.VMEM((tall, cells, KS * LANES), BF16),
            pltpu.VMEM((tall, KS * XROWS, cells), BF16),
            pltpu.VMEM((2 * HALF_TAPS * GROUP, LANES), F32),
            pltpu.VMEM((taps * LANES, LANES), BF16),
            pltpu.VMEM((rows, cells, LANES), BF16),
            pltpu.VMEM((SUM_LANES, LANES), F32),
            pltpu.VMEM((fsdp_count, share, SUM_LANES), F32),
        ],
        compiler_params=pltpu.CompilerParams(vmem_limit_bytes=52 * 1024 * 1024),
        name="section",
    )(
        neighbours, fields, cotangent, above, below,
        far0, far1, close0, close1, edge, *pieces,
    )

    held = keep + swapped(send, "fsdp", lambda i: i ^ 1)
    half = space % 2
    distance = 2
    while held.shape[0] > 1:
        pairs = held.reshape(held.shape[0] // 2, 2, 2, share, HALF_SUM)
        sent = narrowed(pairs[:, 1], half)
        held = pairs[:, 0] + swapped(sent, "fsdp", lambda i: i ^ distance).astype(F32)
        distance *= 2
    held = held[0, 0] + swapped(held[0, 1], "space", lambda i: i ^ 1)
    distance = 2
    while distance * 4 < space_count:
        held = held + swapped(held, "space", lambda i: i ^ distance)
        distance *= 2
    rounded = narrowed(jnp.stack([held]), half)[0]
    others = [swapped(rounded, "space", lambda i, k=k: i ^ (distance * k)) for k in (1, 2, 3)]
    total = (rounded.astype(F32) + others[0].astype(F32)) + (
        others[1].astype(F32) + others[2].astype(F32)
    )
    exact = total[:, BIAS_AT : BIAS_AT + 1] + total[:, BIAS_AT + 1 : BIAS_AT + 2]
    total = jnp.where(bias_lane(total.shape, half, BIAS_AT), exact, total)
    total = jnp.where(bias_lane(total.shape, half, BIAS_AT + 1), 0.0, total)
    squares = jnp.broadcast_to(jnp.sum(total * total, 0, keepdims=True), (8, HALF_SUM))
    squares_beside = swapped(squares, "space", lambda i: i ^ 1)
    squares_beside, total = lax.optimization_barrier((squares_beside, total))
    total_beside = swapped(total, "space", lambda i: i ^ 1)
    squares = squares + squares_beside
    distance = 1
    while distance * 2 < fsdp_count:
        squares = squares + swapped(squares, "fsdp", lambda i: i ^ distance)
        distance *= 2
    all_squares = [squares, swapped(squares, "fsdp", lambda i: i ^ distance)]
    weight_step, bias_step = pl.pallas_call(
        functools.partial(scale_kernel, taps * GROUP * chans + chans),
        out_shape=(
            jax.ShapeDtypeStruct((KS, KS, GROUP, share), F32),
            jax.ShapeDtypeStruct((1, share), F32),
        ),
        in_specs=[VMEM] * 4,
        out_specs=(VMEM, VMEM),
        compiler_params=SMALL,
        name="scale",
    )(total, total_beside, *all_squares)
    return (activations, weight_step, bias_step[0])


def solution(mesh):
    return jax.shard_map(
        per_device,
        mesh=mesh,
        in_specs=(
            P("space", "fsdp", None, None),
            P(None, None, None, "fsdp"),
            P("fsdp"),
            P("space", "fsdp", None, None),
            P("space", None),
        ),
        out_specs=(P("space", "fsdp", None, None), P(None, None, None, "fsdp"), P("fsdp")),
        check_vma=False,
    )
```

```python
import functools

import jax
import jax.numpy as jnp
from jax import lax
from jax.experimental import pallas as pl
from jax.experimental.pallas import tpu as pltpu
from jax.sharding import PartitionSpec as P

GROUP = 40
KS = 5
RIM = 2
LANES = 256
HALF = 64
HALF_TAPS = 13
PIECE_ROWS = 528
SUM_LANES = 1024
STEP = 4
HALF_SUM = SUM_LANES // 2
BIAS_AT = KS * KS * GROUP - HALF_SUM
XROWS = 208
VMEM = pl.BlockSpec(memory_space=pltpu.VMEM)
ANY = pl.BlockSpec(memory_space=pl.ANY)
SMEM = pl.BlockSpec(memory_space=pltpu.SMEM)
F32 = jnp.float32
SMALL = pltpu.CompilerParams(vmem_limit_bytes=12 * 1024 * 1024)
BF16 = jnp.bfloat16


def swapped(value, axis, partner):
    count = lax.axis_size(axis)
    pairs = [(i, partner(i)) for i in range(count)]
    return lax.ppermute(value, axis, [p for p in pairs if 0 <= p[1] < count])


def hop_pairs(value, distance, parity):
    def partner(i):
        return i + distance if (i // distance) % 2 == parity else i - distance

    return swapped(value, "space", partner)


def main_kernel(
    piece_count, near, fields_far, cot_far, above, below, far0, far1, close0, close1, *rest
):
    pieces = rest[:piece_count]
    act_far, keep, send = rest[piece_count : piece_count + 3]
    fields, cot, act, sems, pool_l, pool_r, edges, xf, xs, xst, wc, wd, g, gd, shares = rest[piece_count + 3 :]
    fields_in = pltpu.make_async_copy(fields_far, fields, sems.at[0])
    cot_in = pltpu.make_async_copy(cot_far, cot, sems.at[1])
    fields_in.start()
    cot_in.start()
    tiles, rows, side, chans = fields.shape
    tall = rows + 2 * RIM
    cells = tiles * side
    fsdp_count = lax.axis_size("fsdp")
    fsdp = lax.axis_index("fsdp")
    space = lax.axis_index("space")
    far_odd = lax.rem(lax.div(space, 2), 2) == 1
    close_odd = lax.rem(space, 2) == 1
    share = chans // fsdp_count

    lined = jnp.concatenate([p[...] for p in pieces], axis=1)
    owner = []
    for i in range(piece_count):
        if piece_count == fsdp_count and fsdp_count != 4:
            owner.append(i)
        else:
            owner.append((fsdp, 3 - fsdp, fsdp ^ 1, fsdp ^ 2)[i])
    from_lane = lax.broadcasted_iota(jnp.int32, (128, LANES), 0)
    to_lane = lax.broadcasted_iota(jnp.int32, (128, LANES), 1)
    for half in range(2):
        picks = []
        for i in range(piece_count):
            inside = from_lane - half * HALF
            valid = (inside >= 0) & (inside < share) & (to_lane == owner[i] * share + inside)
            picks.append(jnp.where(valid, 1.0, 0.0).astype(BF16))
        full = jnp.dot(lined, jnp.concatenate(picks, axis=0), preferred_element_type=F32)
        wc[half * HALF_TAPS * GROUP : (half + 1) * HALF_TAPS * GROUP, :] = full[: HALF_TAPS * GROUP]
    group_count = chans // GROUP
    group_of = lax.broadcasted_iota(jnp.int32, (GROUP, LANES), 1) // GROUP
    taps = KS * KS
    for tap in range(taps):
        one = wc[tap * GROUP : (tap + 1) * GROUP]
        blocks = [jnp.where(group_of == k, one, 0.0) for k in range(group_count)]
        if tap == taps // 2:
            blocks.append(wc[taps * GROUP : taps * GROUP + 8])
        else:
            blocks.append(jnp.zeros((8, LANES), F32))
        blocks.append(jnp.zeros((LANES - chans - 8, LANES), F32))
        wd[tap * LANES : (tap + 1) * LANES] = jnp.concatenate(blocks, axis=0).astype(BF16)

    zero_side = jnp.zeros((tall, RIM, LANES), F32)
    zero_slot = 4 * tiles
    pool_l[zero_slot] = zero_side
    pool_r[zero_slot] = zero_side
    for t in range(tiles):
        lo, hi = far0[t].astype(F32), far1[t].astype(F32)
        pool_l[tiles + t, :, :, :chans] = jnp.where(far_odd, lo, hi)
        pool_r[2 * tiles + t, :, :, :chans] = jnp.where(far_odd, hi, lo)
        lo = close0[t * tall : (t + 1) * tall].astype(F32)
        hi = close1[t * tall : (t + 1) * tall].astype(F32)
        pool_l[2 * tiles + t, :, :, :chans] = jnp.where(close_odd, lo, hi)
        pool_r[tiles + t, :, :, :chans] = jnp.where(close_odd, hi, lo)
    lo = close0[tiles * tall : tiles * tall + RIM].astype(F32)
    hi = close1[tiles * tall : tiles * tall + RIM].astype(F32)
    pool_l[tiles - 1, :RIM, :, :chans] = jnp.where(close_odd, lo, hi)
    pool_r[3 * tiles, rows + RIM :, :, :chans] = jnp.where(close_odd, hi, lo)

    lo = close0[tiles * tall + RIM :].astype(F32)
    hi = close1[tiles * tall + RIM :].astype(F32)
    edges[0, :, :, :chans] = jnp.where(close_odd, lo, hi)
    edges[1, :, :, :chans] = jnp.where(close_odd, hi, lo)
    edge_north = jnp.stack([edges[0, :, r, :chans] for r in range(RIM)])
    edge_south = jnp.stack([edges[1, :, r, :chans] for r in range(RIM)])
    fields_in.wait()

    lane = lax.broadcasted_iota(jnp.int32, (tiles, side + 16, 128), 2)
    one_behind = jnp.where(lane == chans - 128, 1.0, 0.0).astype(F32)
    for r in range(tall):
        xf[r, :, :, 128:] = one_behind
    for t in range(tiles):
        top, bottom = above[t].astype(F32), below[t].astype(F32)
        centre = fields[t].astype(F32)
        for part, first in ((top, 0), (centre, RIM), (bottom, RIM + rows)):
            length = part.shape[0]
            pool_l[3 * tiles + t, first : first + length, :, :chans] = part[:, side - RIM :]
            pool_r[t, first : first + length, :, :chans] = part[:, :RIM]
        xf[RIM : RIM + rows, t, 8 : 8 + side, :chans] = centre
        north = edge_north if t == 0 else above[t - 1].astype(F32)
        south = edge_south if t == tiles - 1 else below[t + 1].astype(F32)
        north = jnp.where(near[t, 0] >= 0, north, 0.0)
        south = jnp.where(near[t, 1] >= 0, south, 0.0)
        xf[:RIM, t, 8 : 8 + side, :chans] = jnp.where(fsdp == 0, north, top)
        xf[RIM + rows :, t, 8 : 8 + side, :chans] = jnp.where(fsdp == fsdp_count - 1, south, bottom)

    def slot(tile_id, first):
        return jnp.where(tile_id < 0, zero_slot, jnp.clip(tile_id - first * tiles, 0, zero_slot))

    for t in range(tiles):
        for pool, column, first, beside, up, down in (
            (pool_l, 6, space - 3, near[t, 2], near[t, 4], near[t, 6]),
            (pool_r, 8 + side, space, near[t, 3], near[t, 5], near[t, 7]),
        ):
            mid = slot(beside, first)
            top = jnp.where(fsdp == 0, slot(up, first), mid)
            bottom = jnp.where(fsdp == fsdp_count - 1, slot(down, first), mid)
            into = pl.ds(column, RIM)
            xf[RIM : RIM + rows, t, into, :chans] = pool[mid, RIM : RIM + rows, :, :chans]
            xf[:RIM, t, into, :chans] = pool[top, :RIM, :, :chans]
            xf[RIM + rows :, t, into, :chans] = pool[bottom, RIM + rows :, :, :chans]

    def shift(some_rows):
        for r in some_rows:
            for b in range(KS):
                piece = xf[r, :, 6 + b : 6 + b + side, :].astype(BF16).reshape(cells, LANES)
                xs[r, :, b * LANES : (b + 1) * LANES] = piece
                xst[r, b * XROWS : (b + 1) * XROWS, :] = piece.T[:XROWS]

    cot_in.wait()
    act_out = []
    step = min(STEP, rows)
    reach = step + KS - 1
    shift(range(reach))
    for r0 in range(0, rows, step):
        if r0 + step < rows:
            shift(range(r0 + reach, r0 + reach + step))
        total = None
        for a in range(KS):
            left = xs[r0 + a : r0 + a + step].reshape(step * cells, KS * LANES)
            right = wd[a * KS * LANES : (a + 1) * KS * LANES]
            part = jnp.dot(left, right, preferred_element_type=F32)
            total = part if total is None else total + part
        total = total.reshape(step, tiles, side, LANES)
        for t in range(tiles):
            pre = total[:, t, :, :chans]
            logistic = 1.0 / (1.0 + jnp.exp(-pre))
            act[t, r0 : r0 + step] = (pre * logistic).astype(BF16)
            up = cot[t, r0 : r0 + step].astype(F32)
            g[r0 : r0 + step, t * side : (t + 1) * side, :chans] = (
                up * logistic * (1.0 + pre * (1.0 - logistic))
            ).astype(BF16)

        chunk = pl.ds(r0, step)
        act_out.append(
            pltpu.make_async_copy(act.at[:, chunk], act_far.at[:, chunk], sems.at[2 + r0 // step])
        )
        act_out[-1].start()

    right = g[...].reshape(rows * cells, LANES)
    for a in range(KS):
        left = jnp.concatenate([xst[r + a] for r in range(rows)], axis=1)
        part = jnp.dot(left, right, preferred_element_type=F32)
        for b in range(KS):
            fold = jnp.zeros((GROUP, LANES), F32)
            for k in range(group_count):
                first = b * XROWS + k * GROUP
                fold = jnp.where(group_of == k, part[first : first + GROUP], fold)
            first = (a * KS + b) * GROUP
            gd[first : first + GROUP] = fold
        if a == 0:
            gd[taps * GROUP : taps * GROUP + 8] = part[chans : chans + 8]
            gd[taps * GROUP + 8 :] = jnp.zeros((SUM_LANES - taps * GROUP - 8, LANES), F32)
    turned = gd[...].T
    for i in range(fsdp_count):
        shares[i] = turned[i * share : (i + 1) * share]
    for i in range(fsdp_count // 2):
        for into, whose in ((keep, fsdp ^ (2 * i)), (send, fsdp ^ (2 * i + 1))):
            low, high = shares[whose, :, :HALF_SUM], shares[whose, :, HALF_SUM:]
            into[i, 0] = jnp.where(close_odd, high, low)
            into[i, 1] = jnp.where(close_odd, low, high)
    for copy in act_out:
        copy.wait()


def bias_lane(shape, half, at):
    lane = lax.broadcasted_iota(jnp.int32, shape, len(shape) - 1)
    return (lane == at) & (half == 1)


def narrowed(value, half):
    lead = value.shape[:-2]
    index = lax.broadcasted_iota(jnp.int32, value.shape, len(lead) - 1)
    whose = index ^ half
    bias_sum = value[..., BIAS_AT : BIAS_AT + 1] + value[..., BIAS_AT + 1 : BIAS_AT + 2]
    bias_low = bias_sum - lax.reduce_precision(bias_sum, 8, 7)
    value = jnp.where(bias_lane(value.shape, whose, BIAS_AT), bias_sum, value)
    return jnp.where(bias_lane(value.shape, whose, BIAS_AT + 1), bias_low, value).astype(BF16)


def scale_kernel(entries, own, beside, *rest):
    squares, (weight_out, bias_out) = rest[:-2], rest[-2:]
    odd = lax.rem(lax.axis_index("space"), 2) == 1
    count = KS * KS * GROUP
    share = own.shape[0]
    sums = [value[0:1, :] for value in squares]
    while len(sums) > 1:
        sums = [a + b for a, b in zip(sums[::2], sums[1::2])]
    scaling = lax.rsqrt(jnp.sum(sums[0], axis=1, keepdims=True) / entries + 1e-06)
    low = jnp.where(odd, beside[...], own[...])
    high = jnp.where(odd, own[...], beside[...])
    whole = jnp.concatenate([low, high], axis=1) * scaling
    whole = jnp.concatenate([whole, jnp.zeros((128 - share, SUM_LANES), F32)], axis=0)
    turned = whole.T
    weight_out[...] = turned[:count, :share].reshape(weight_out.shape)
    bias_out[...] = turned[count : count + 1, :share]


def rim_kernel(
    fields, ends_outward, ends_core, rows_outward, rows_core, west, east, rims, sides, sems
):
    rows, side = fields.shape[1:3]
    even = lax.rem(lax.axis_index("fsdp"), 2) == 0
    copies = [
        pltpu.make_async_copy(fields.at[:, pl.ds(0, RIM)], rims.at[0], sems.at[0]),
        pltpu.make_async_copy(fields.at[:, pl.ds(rows - RIM, RIM)], rims.at[1], sems.at[1]),
        pltpu.make_async_copy(fields.at[:, :, pl.ds(0, 16)], sides.at[0], sems.at[2]),
        pltpu.make_async_copy(fields.at[:, :, pl.ds(side - 16, 16)], sides.at[1], sems.at[3]),
    ]
    for copy in copies:
        copy.start()
    for copy in copies:
        copy.wait()

    def give(first_ends, first_rows, last_ends, last_rows):
        for i, (ends, outer) in enumerate(((first_ends, first_rows), (last_ends, last_rows))):
            outer[...] = rims[i]
            ends[:, :, :RIM] = rims[i, :, :, :RIM]
            ends[:, :, RIM:] = rims[i, :, :, side - RIM :]

    @pl.when(even)
    def _():
        give(ends_outward, rows_outward, ends_core, rows_core)

    @pl.when(jnp.logical_not(even))
    def _():
        give(ends_core, rows_core, ends_outward, rows_outward)

    west[...] = sides[0, :, :, :RIM]
    east[...] = sides[1, :, :, 16 - RIM :]


def pack_kernel(weight, bias, packed, wide):
    share = weight.shape[2]
    high = KS * KS - HALF_TAPS
    wide[...] = jnp.zeros(wide.shape, F32)
    wide[: HALF_TAPS * GROUP, :share] = weight[:HALF_TAPS].astype(F32).reshape(-1, share)
    wide[: high * GROUP, HALF : HALF + share] = weight[HALF_TAPS:].astype(F32).reshape(-1, share)
    wide[high * GROUP : high * GROUP + 1, HALF : HALF + share] = bias[...].astype(F32)
    packed[...] = wide[...].astype(BF16)


def per_device(fields, weight, bias, cotangent, neighbours):
    tiles, rows, side, chans = fields.shape
    fsdp_count = lax.axis_size("fsdp")
    space_count = lax.axis_size("space")
    fsdp = lax.axis_index("fsdp")
    space = lax.axis_index("space")
    share = chans // fsdp_count
    taps = KS * KS
    tall = rows + 2 * RIM

    even = fsdp % 2 == 0

    def outward(i):
        return (i + 1) % fsdp_count if i % 2 else (i - 1) % fsdp_count

    def joined(name_outward, name_core):
        up = jnp.where(even, name_outward, name_core)
        return up, jnp.where(even, name_core, name_outward)

    def inward(i):
        return i ^ 1

    ends = jax.ShapeDtypeStruct((tiles, RIM, 2 * RIM, chans), BF16)
    rim = jax.ShapeDtypeStruct((tiles, RIM, side, chans), BF16)
    columns = jax.ShapeDtypeStruct((tiles, rows, RIM, chans), BF16)
    ends_outward, ends_core, rows_outward, rows_core, west_own, east_own = pl.pallas_call(
        rim_kernel,
        out_shape=(ends, ends, rim, rim, columns, columns),
        in_specs=[ANY],
        out_specs=(VMEM,) * 6,
        scratch_shapes=[
            pltpu.VMEM((2, tiles, RIM, side, chans), BF16),
            pltpu.VMEM((2, tiles, rows, 16, chans), BF16),
            pltpu.SemaphoreType.DMA((4,)),
        ],
        compiler_params=SMALL,
        name="rims",
    )(fields)
    packed = pl.pallas_call(
        pack_kernel,
        out_shape=jax.ShapeDtypeStruct((PIECE_ROWS, 128), BF16),
        in_specs=[VMEM] * 2,
        out_specs=VMEM,
        scratch_shapes=[pltpu.VMEM((PIECE_ROWS, 128), F32)],
        compiler_params=SMALL,
        name="pack",
    )(weight.reshape(taps, GROUP, share), bias[None, :])
    ends_outward = swapped(ends_outward, "fsdp", outward)
    ends_core = swapped(ends_core, "fsdp", inward)
    from_outward = swapped(rows_outward, "fsdp", outward)
    from_core = swapped(rows_core, "fsdp", inward)
    if fsdp_count == 4:
        packed_out = swapped(packed, "fsdp", outward)
        packed_core = swapped(packed, "fsdp", inward)
    ends_above, ends_below = joined(ends_outward, ends_core)

    west = jnp.concatenate([ends_above[:, :, :RIM], west_own, ends_below[:, :, :RIM]], 1)
    east = jnp.concatenate([ends_above[:, :, RIM:], east_own, ends_below[:, :, RIM:]], 1)
    far_odd = (space // 2) % 2 == 1
    close_odd = space % 2 == 1
    far0 = hop_pairs(jnp.where(far_odd, west, east), 2, 0)
    far1 = hop_pairs(jnp.where(far_odd, east, west), 2, 1)
    if fsdp_count == 4:
        far0, far1, packed_out = lax.optimization_barrier((far0, far1, packed_out))
        packed_last = swapped(packed_out, "fsdp", inward)
    far0, far1, from_outward, from_core = lax.optimization_barrier(
        (far0, far1, from_outward, from_core)
    )
    above, below = joined(from_outward, from_core)
    east_far = jnp.where(far_odd, far0, far1)[tiles - 1, :RIM]
    west_far = jnp.where(far_odd, far1, far0)[0, rows + RIM :]
    flat_side = (tiles * tall, RIM, chans)
    edge_east = jnp.swapaxes(above[tiles - 1], 0, 1)
    edge_west = jnp.swapaxes(below[0], 0, 1)
    to_east = jnp.concatenate([east.reshape(flat_side), east_far, edge_east], 0)
    to_west = jnp.concatenate([west.reshape(flat_side), west_far, edge_west], 0)
    close0 = hop_pairs(jnp.where(close_odd, to_west, to_east), 1, 0)
    close1 = hop_pairs(jnp.where(close_odd, to_east, to_west), 1, 1)
    if fsdp_count == 4:
        pieces = [packed, packed_out, packed_core, packed_last]
    else:
        gathered = lax.all_gather(packed, "fsdp")
        pieces = [gathered[i] for i in range(fsdp_count)]

    cells = tiles * side
    part = jax.ShapeDtypeStruct((fsdp_count // 2, 2, share, HALF_SUM), F32)
    activations, keep, send = pl.pallas_call(
        functools.partial(main_kernel, len(pieces)),
        out_shape=(jax.ShapeDtypeStruct(fields.shape, BF16), part, part),
        in_specs=[SMEM, ANY, ANY] + [VMEM] * (6 + len(pieces)),
        out_specs=(ANY, VMEM, VMEM),
        scratch_shapes=[
            pltpu.VMEM(fields.shape, BF16),
            pltpu.VMEM(fields.shape, BF16),
            pltpu.VMEM(fields.shape, BF16),
            pltpu.SemaphoreType.DMA((2 + rows // min(STEP, rows),)),
            pltpu.VMEM((4 * tiles + 1, tall, RIM, LANES), F32),
            pltpu.VMEM((4 * tiles + 1, tall, RIM, LANES), F32),
            pltpu.VMEM((2, side, RIM, LANES), F32),
            pltpu.VMEM((tall, tiles, side + 16, LANES), F32),
            pltpu.VMEM((tall, cells, KS * LANES), BF16),
            pltpu.VMEM((tall, KS * XROWS, cells), BF16),
            pltpu.VMEM((2 * HALF_TAPS * GROUP, LANES), F32),
            pltpu.VMEM((taps * LANES, LANES), BF16),
            pltpu.VMEM((rows, cells, LANES), BF16),
            pltpu.VMEM((SUM_LANES, LANES), F32),
            pltpu.VMEM((fsdp_count, share, SUM_LANES), F32),
        ],
        compiler_params=pltpu.CompilerParams(vmem_limit_bytes=52 * 1024 * 1024),
        name="section",
    )(
        neighbours, fields, cotangent, above, below,
        far0, far1, close0, close1, *pieces,
    )

    held = keep + swapped(send, "fsdp", lambda i: i ^ 1)
    half = space % 2
    distance = 2
    while held.shape[0] > 1:
        pairs = held.reshape(held.shape[0] // 2, 2, 2, share, HALF_SUM)
        sent = narrowed(pairs[:, 1], half)
        held = pairs[:, 0] + swapped(sent, "fsdp", lambda i: i ^ distance).astype(F32)
        distance *= 2
    held = held[0, 0] + swapped(held[0, 1], "space", lambda i: i ^ 1)
    distance = 2
    while distance * 4 < space_count:
        held = held + swapped(held, "space", lambda i: i ^ distance)
        distance *= 2
    rounded = narrowed(jnp.stack([held]), half)[0]
    others = [swapped(rounded, "space", lambda i, k=k: i ^ (distance * k)) for k in (1, 2, 3)]
    total = (rounded.astype(F32) + others[0].astype(F32)) + (
        others[1].astype(F32) + others[2].astype(F32)
    )
    exact = total[:, BIAS_AT : BIAS_AT + 1] + total[:, BIAS_AT + 1 : BIAS_AT + 2]
    total = jnp.where(bias_lane(total.shape, half, BIAS_AT), exact, total)
    total = jnp.where(bias_lane(total.shape, half, BIAS_AT + 1), 0.0, total)
    squares = jnp.broadcast_to(jnp.sum(total * total, 0, keepdims=True), (8, HALF_SUM))
    total_beside = swapped(total, "space", lambda i: i ^ 1)
    distance = 1
    while distance * 2 < fsdp_count:
        squares = squares + swapped(squares, "fsdp", lambda i: i ^ distance)
        distance *= 2
    both = [
        (s * fsdp_count + q, (s ^ 1) * fsdp_count + (q ^ distance))
        for s in range(space_count)
        for q in range(fsdp_count)
    ]
    all_squares = [
        squares,
        swapped(squares, "space", lambda i: i ^ 1),
        swapped(squares, "fsdp", lambda i: i ^ distance),
        lax.ppermute(squares, ("space", "fsdp"), both),
    ]
    weight_step, bias_step = pl.pallas_call(
        functools.partial(scale_kernel, taps * GROUP * chans + chans),
        out_shape=(
            jax.ShapeDtypeStruct((KS, KS, GROUP, share), F32),
            jax.ShapeDtypeStruct((1, share), F32),
        ),
        in_specs=[VMEM] * 6,
        out_specs=(VMEM, VMEM),
        compiler_params=SMALL,
        name="scale",
    )(total, total_beside, *all_squares)
    return (activations, weight_step, bias_step[0])


def solution(mesh):
    return jax.shard_map(
        per_device,
        mesh=mesh,
        in_specs=(
            P("space", "fsdp", None, None),
            P(None, None, None, "fsdp"),
            P("fsdp"),
            P("space", "fsdp", None, None),
            P("space", None),
        ),
        out_specs=(P("space", "fsdp", None, None), P(None, None, None, "fsdp"), P("fsdp")),
        check_vma=False,
    )
```

```python
import functools

import jax
import jax.numpy as jnp
from jax import lax
from jax.experimental import pallas as pl
from jax.experimental.pallas import tpu as pltpu
from jax.sharding import PartitionSpec as P

GROUP = 40
KS = 5
RIM = 2
LANES = 256
HALF = 64
HALF_TAPS = 13
PIECE_ROWS = 528
SUM_LANES = 1024
STEP = 4
HALF_SUM = SUM_LANES // 2
BIAS_AT = KS * KS * GROUP - HALF_SUM
XROWS = 208
VMEM = pl.BlockSpec(memory_space=pltpu.VMEM)
ANY = pl.BlockSpec(memory_space=pl.ANY)
SMEM = pl.BlockSpec(memory_space=pltpu.SMEM)
F32 = jnp.float32
SMALL = pltpu.CompilerParams(vmem_limit_bytes=12 * 1024 * 1024)
BF16 = jnp.bfloat16


def swapped(value, axis, partner):
    count = lax.axis_size(axis)
    pairs = [(i, partner(i)) for i in range(count)]
    return lax.ppermute(value, axis, [p for p in pairs if 0 <= p[1] < count])


def hop_pairs(value, distance, parity):
    def partner(i):
        return i + distance if (i // distance) % 2 == parity else i - distance

    return swapped(value, "space", partner)


def expand_kernel(chans, *refs):
    *pieces, wd, wc = refs
    piece_count = len(pieces)
    fsdp_count = lax.axis_size("fsdp")
    fsdp = lax.axis_index("fsdp")
    share = chans // fsdp_count

    lined = jnp.concatenate([p[...] for p in pieces], axis=1)
    owner = []
    for i in range(piece_count):
        if piece_count == fsdp_count and fsdp_count != 4:
            owner.append(i)
        else:
            owner.append((fsdp, 3 - fsdp, fsdp ^ 1, fsdp ^ 2)[i])
    from_lane = lax.broadcasted_iota(jnp.int32, (128, LANES), 0)
    to_lane = lax.broadcasted_iota(jnp.int32, (128, LANES), 1)
    for half in range(2):
        picks = []
        for i in range(piece_count):
            inside = from_lane - half * HALF
            valid = (inside >= 0) & (inside < share) & (to_lane == owner[i] * share + inside)
            picks.append(jnp.where(valid, 1.0, 0.0).astype(BF16))
        full = jnp.dot(lined, jnp.concatenate(picks, axis=0), preferred_element_type=F32)
        wc[half * HALF_TAPS * GROUP : (half + 1) * HALF_TAPS * GROUP, :] = full[: HALF_TAPS * GROUP]
    group_count = chans // GROUP
    group_of = lax.broadcasted_iota(jnp.int32, (GROUP, LANES), 1) // GROUP
    taps = KS * KS
    for tap in range(taps):
        one = wc[tap * GROUP : (tap + 1) * GROUP]
        blocks = [jnp.where(group_of == k, one, 0.0) for k in range(group_count)]
        if tap == taps // 2:
            blocks.append(wc[taps * GROUP : taps * GROUP + 8])
        else:
            blocks.append(jnp.zeros((8, LANES), F32))
        blocks.append(jnp.zeros((LANES - chans - 8, LANES), F32))
        wd[tap * LANES : (tap + 1) * LANES] = jnp.concatenate(blocks, axis=0).astype(BF16)


def main_kernel(
    near, fields_far, cot_far, above, below, far0, far1, close0, close1, wd,
    act_far, keep, send, fields, cot, act, sems, pool_l, pool_r, edges, xf, xs, xst, g, gd, shares,
):
    fields_in = pltpu.make_async_copy(fields_far, fields, sems.at[0])
    cot_in = pltpu.make_async_copy(cot_far, cot, sems.at[1])
    fields_in.start()
    cot_in.start()
    tiles, rows, side, chans = fields.shape
    tall = rows + 2 * RIM
    cells = tiles * side
    fsdp_count = lax.axis_size("fsdp")
    fsdp = lax.axis_index("fsdp")
    space = lax.axis_index("space")
    far_odd = lax.rem(lax.div(space, 2), 2) == 1
    close_odd = lax.rem(space, 2) == 1
    share = chans // fsdp_count

    group_count = chans // GROUP
    group_of = lax.broadcasted_iota(jnp.int32, (GROUP, LANES), 1) // GROUP
    taps = KS * KS

    zero_side = jnp.zeros((tall, RIM, LANES), F32)
    zero_slot = 4 * tiles
    pool_l[zero_slot] = zero_side
    pool_r[zero_slot] = zero_side
    for t in range(tiles):
        lo, hi = far0[t].astype(F32), far1[t].astype(F32)
        pool_l[tiles + t, :, :, :chans] = jnp.where(far_odd, lo, hi)
        pool_r[2 * tiles + t, :, :, :chans] = jnp.where(far_odd, hi, lo)
        lo = close0[t * tall : (t + 1) * tall].astype(F32)
        hi = close1[t * tall : (t + 1) * tall].astype(F32)
        pool_l[2 * tiles + t, :, :, :chans] = jnp.where(close_odd, lo, hi)
        pool_r[tiles + t, :, :, :chans] = jnp.where(close_odd, hi, lo)
    lo = close0[tiles * tall : tiles * tall + RIM].astype(F32)
    hi = close1[tiles * tall : tiles * tall + RIM].astype(F32)
    pool_l[tiles - 1, :RIM, :, :chans] = jnp.where(close_odd, lo, hi)
    pool_r[3 * tiles, rows + RIM :, :, :chans] = jnp.where(close_odd, hi, lo)

    lo = close0[tiles * tall + RIM :].astype(F32)
    hi = close1[tiles * tall + RIM :].astype(F32)
    edges[0, :, :, :chans] = jnp.where(close_odd, lo, hi)
    edges[1, :, :, :chans] = jnp.where(close_odd, hi, lo)
    edge_north = jnp.stack([edges[0, :, r, :chans] for r in range(RIM)])
    edge_south = jnp.stack([edges[1, :, r, :chans] for r in range(RIM)])
    fields_in.wait()

    lane = lax.broadcasted_iota(jnp.int32, (tiles, side + 16, 128), 2)
    one_behind = jnp.where(lane == chans - 128, 1.0, 0.0).astype(F32)
    for r in range(tall):
        xf[r, :, :, 128:] = one_behind
    for t in range(tiles):
        top, bottom = above[t].astype(F32), below[t].astype(F32)
        centre = fields[t].astype(F32)
        for part, first in ((top, 0), (centre, RIM), (bottom, RIM + rows)):
            length = part.shape[0]
            pool_l[3 * tiles + t, first : first + length, :, :chans] = part[:, side - RIM :]
            pool_r[t, first : first + length, :, :chans] = part[:, :RIM]
        xf[RIM : RIM + rows, t, 8 : 8 + side, :chans] = centre
        north = edge_north if t == 0 else above[t - 1].astype(F32)
        south = edge_south if t == tiles - 1 else below[t + 1].astype(F32)
        north = jnp.where(near[t, 0] >= 0, north, 0.0)
        south = jnp.where(near[t, 1] >= 0, south, 0.0)
        xf[:RIM, t, 8 : 8 + side, :chans] = jnp.where(fsdp == 0, north, top)
        xf[RIM + rows :, t, 8 : 8 + side, :chans] = jnp.where(fsdp == fsdp_count - 1, south, bottom)

    def slot(tile_id, first):
        return jnp.where(tile_id < 0, zero_slot, jnp.clip(tile_id - first * tiles, 0, zero_slot))

    for t in range(tiles):
        for pool, column, first, beside, up, down in (
            (pool_l, 6, space - 3, near[t, 2], near[t, 4], near[t, 6]),
            (pool_r, 8 + side, space, near[t, 3], near[t, 5], near[t, 7]),
        ):
            mid = slot(beside, first)
            top = jnp.where(fsdp == 0, slot(up, first), mid)
            bottom = jnp.where(fsdp == fsdp_count - 1, slot(down, first), mid)
            into = pl.ds(column, RIM)
            xf[RIM : RIM + rows, t, into, :chans] = pool[mid, RIM : RIM + rows, :, :chans]
            xf[:RIM, t, into, :chans] = pool[top, :RIM, :, :chans]
            xf[RIM + rows :, t, into, :chans] = pool[bottom, RIM + rows :, :, :chans]

    def shift(some_rows):
        for r in some_rows:
            for b in range(KS):
                piece = xf[r, :, 6 + b : 6 + b + side, :].astype(BF16).reshape(cells, LANES)
                xs[r, :, b * LANES : (b + 1) * LANES] = piece
                xst[r, b * XROWS : (b + 1) * XROWS, :] = piece.T[:XROWS]

    cot_in.wait()
    act_out = []
    step = min(STEP, rows)
    reach = step + KS - 1
    shift(range(reach))
    for r0 in range(0, rows, step):
        if r0 + step < rows:
            shift(range(r0 + reach, r0 + reach + step))
        total = None
        for a in range(KS):
            left = xs[r0 + a : r0 + a + step].reshape(step * cells, KS * LANES)
            right = wd[a * KS * LANES : (a + 1) * KS * LANES]
            part = jnp.dot(left, right, preferred_element_type=F32)
            total = part if total is None else total + part
        total = total.reshape(step, tiles, side, LANES)
        for t in range(tiles):
            pre = total[:, t, :, :chans]
            logistic = 1.0 / (1.0 + jnp.exp(-pre))
            act[t, r0 : r0 + step] = (pre * logistic).astype(BF16)
            up = cot[t, r0 : r0 + step].astype(F32)
            g[r0 : r0 + step, t * side : (t + 1) * side, :chans] = (
                up * logistic * (1.0 + pre * (1.0 - logistic))
            ).astype(BF16)

        chunk = pl.ds(r0, step)
        act_out.append(
            pltpu.make_async_copy(act.at[:, chunk], act_far.at[:, chunk], sems.at[2 + r0 // step])
        )
        act_out[-1].start()

    right = g[...].reshape(rows * cells, LANES)
    for a in range(KS):
        left = jnp.concatenate([xst[r + a] for r in range(rows)], axis=1)
        part = jnp.dot(left, right, preferred_element_type=F32)
        for b in range(KS):
            fold = jnp.zeros((GROUP, LANES), F32)
            for k in range(group_count):
                first = b * XROWS + k * GROUP
                fold = jnp.where(group_of == k, part[first : first + GROUP], fold)
            first = (a * KS + b) * GROUP
            gd[first : first + GROUP] = fold
        if a == 0:
            gd[taps * GROUP : taps * GROUP + 8] = part[chans : chans + 8]
            gd[taps * GROUP + 8 :] = jnp.zeros((SUM_LANES - taps * GROUP - 8, LANES), F32)
    turned = gd[...].T
    for i in range(fsdp_count):
        shares[i] = turned[i * share : (i + 1) * share]
    for i in range(fsdp_count // 2):
        for into, whose in ((keep, fsdp ^ (2 * i)), (send, fsdp ^ (2 * i + 1))):
            low, high = shares[whose, :, :HALF_SUM], shares[whose, :, HALF_SUM:]
            into[i, 0] = jnp.where(close_odd, high, low)
            into[i, 1] = jnp.where(close_odd, low, high)
    for copy in act_out:
        copy.wait()


def bias_lane(shape, half, at):
    lane = lax.broadcasted_iota(jnp.int32, shape, len(shape) - 1)
    return (lane == at) & (half == 1)


def narrowed(value, half):
    lead = value.shape[:-2]
    index = lax.broadcasted_iota(jnp.int32, value.shape, len(lead) - 1)
    whose = index ^ half
    bias_sum = value[..., BIAS_AT : BIAS_AT + 1] + value[..., BIAS_AT + 1 : BIAS_AT + 2]
    bias_low = bias_sum - lax.reduce_precision(bias_sum, 8, 7)
    value = jnp.where(bias_lane(value.shape, whose, BIAS_AT), bias_sum, value)
    return jnp.where(bias_lane(value.shape, whose, BIAS_AT + 1), bias_low, value).astype(BF16)


def scale_kernel(entries, own, beside, *rest):
    squares, (weight_out, bias_out) = rest[:-2], rest[-2:]
    odd = lax.rem(lax.axis_index("space"), 2) == 1
    count = KS * KS * GROUP
    share = own.shape[0]
    sums = [value[0:1, :] for value in squares]
    while len(sums) > 1:
        sums = [a + b for a, b in zip(sums[::2], sums[1::2])]
    scaling = lax.rsqrt(jnp.sum(sums[0], axis=1, keepdims=True) / entries + 1e-06)
    low = jnp.where(odd, beside[...], own[...])
    high = jnp.where(odd, own[...], beside[...])
    whole = jnp.concatenate([low, high], axis=1) * scaling
    whole = jnp.concatenate([whole, jnp.zeros((128 - share, SUM_LANES), F32)], axis=0)
    turned = whole.T
    weight_out[...] = turned[:count, :share].reshape(weight_out.shape)
    bias_out[...] = turned[count : count + 1, :share]


def rim_kernel(
    fields, ends_outward, ends_core, rows_outward, rows_core, west, east, rims, sides, sems
):
    rows, side = fields.shape[1:3]
    even = lax.rem(lax.axis_index("fsdp"), 2) == 0
    copies = [
        pltpu.make_async_copy(fields.at[:, pl.ds(0, RIM)], rims.at[0], sems.at[0]),
        pltpu.make_async_copy(fields.at[:, pl.ds(rows - RIM, RIM)], rims.at[1], sems.at[1]),
        pltpu.make_async_copy(fields.at[:, :, pl.ds(0, 16)], sides.at[0], sems.at[2]),
        pltpu.make_async_copy(fields.at[:, :, pl.ds(side - 16, 16)], sides.at[1], sems.at[3]),
    ]
    for copy in copies:
        copy.start()
    for copy in copies:
        copy.wait()

    def give(first_ends, first_rows, last_ends, last_rows):
        for i, (ends, outer) in enumerate(((first_ends, first_rows), (last_ends, last_rows))):
            outer[...] = rims[i]
            ends[:, :, :RIM] = rims[i, :, :, :RIM]
            ends[:, :, RIM:] = rims[i, :, :, side - RIM :]

    @pl.when(even)
    def _():
        give(ends_outward, rows_outward, ends_core, rows_core)

    @pl.when(jnp.logical_not(even))
    def _():
        give(ends_core, rows_core, ends_outward, rows_outward)

    west[...] = sides[0, :, :, :RIM]
    east[...] = sides[1, :, :, 16 - RIM :]


def pack_kernel(weight, bias, packed, wide):
    share = weight.shape[2]
    high = KS * KS - HALF_TAPS
    wide[...] = jnp.zeros(wide.shape, F32)
    wide[: HALF_TAPS * GROUP, :share] = weight[:HALF_TAPS].astype(F32).reshape(-1, share)
    wide[: high * GROUP, HALF : HALF + share] = weight[HALF_TAPS:].astype(F32).reshape(-1, share)
    wide[high * GROUP : high * GROUP + 1, HALF : HALF + share] = bias[...].astype(F32)
    packed[...] = wide[...].astype(BF16)


def per_device(fields, weight, bias, cotangent, neighbours):
    tiles, rows, side, chans = fields.shape
    fsdp_count = lax.axis_size("fsdp")
    space_count = lax.axis_size("space")
    fsdp = lax.axis_index("fsdp")
    space = lax.axis_index("space")
    share = chans // fsdp_count
    taps = KS * KS
    tall = rows + 2 * RIM

    even = fsdp % 2 == 0

    def outward(i):
        return (i + 1) % fsdp_count if i % 2 else (i - 1) % fsdp_count

    def joined(name_outward, name_core):
        up = jnp.where(even, name_outward, name_core)
        return up, jnp.where(even, name_core, name_outward)

    def inward(i):
        return i ^ 1

    ends = jax.ShapeDtypeStruct((tiles, RIM, 2 * RIM, chans), BF16)
    rim = jax.ShapeDtypeStruct((tiles, RIM, side, chans), BF16)
    columns = jax.ShapeDtypeStruct((tiles, rows, RIM, chans), BF16)
    ends_outward, ends_core, rows_outward, rows_core, west_own, east_own = pl.pallas_call(
        rim_kernel,
        out_shape=(ends, ends, rim, rim, columns, columns),
        in_specs=[ANY],
        out_specs=(VMEM,) * 6,
        scratch_shapes=[
            pltpu.VMEM((2, tiles, RIM, side, chans), BF16),
            pltpu.VMEM((2, tiles, rows, 16, chans), BF16),
            pltpu.SemaphoreType.DMA((4,)),
        ],
        compiler_params=SMALL,
        name="rims",
    )(fields)
    packed = pl.pallas_call(
        pack_kernel,
        out_shape=jax.ShapeDtypeStruct((PIECE_ROWS, 128), BF16),
        in_specs=[VMEM] * 2,
        out_specs=VMEM,
        scratch_shapes=[pltpu.VMEM((PIECE_ROWS, 128), F32)],
        compiler_params=SMALL,
        name="pack",
    )(weight.reshape(taps, GROUP, share), bias[None, :])
    ends_outward = swapped(ends_outward, "fsdp", outward)
    ends_core = swapped(ends_core, "fsdp", inward)
    from_outward = swapped(rows_outward, "fsdp", outward)
    from_core = swapped(rows_core, "fsdp", inward)
    if fsdp_count == 4:
        packed_out = swapped(packed, "fsdp", outward)
        packed_core = swapped(packed, "fsdp", inward)
    ends_above, ends_below = joined(ends_outward, ends_core)

    west = jnp.concatenate([ends_above[:, :, :RIM], west_own, ends_below[:, :, :RIM]], 1)
    east = jnp.concatenate([ends_above[:, :, RIM:], east_own, ends_below[:, :, RIM:]], 1)
    far_odd = (space // 2) % 2 == 1
    close_odd = space % 2 == 1
    far0 = hop_pairs(jnp.where(far_odd, west, east), 2, 0)
    far1 = hop_pairs(jnp.where(far_odd, east, west), 2, 1)
    if fsdp_count == 4:
        far0, far1, packed_out = lax.optimization_barrier((far0, far1, packed_out))
        packed_last = swapped(packed_out, "fsdp", inward)
    far0, far1, from_outward, from_core = lax.optimization_barrier(
        (far0, far1, from_outward, from_core)
    )
    above, below = joined(from_outward, from_core)
    east_far = jnp.where(far_odd, far0, far1)[tiles - 1, :RIM]
    west_far = jnp.where(far_odd, far1, far0)[0, rows + RIM :]
    flat_side = (tiles * tall, RIM, chans)
    edge_east = jnp.swapaxes(above[tiles - 1], 0, 1)
    edge_west = jnp.swapaxes(below[0], 0, 1)
    to_east = jnp.concatenate([east.reshape(flat_side), east_far, edge_east], 0)
    to_west = jnp.concatenate([west.reshape(flat_side), west_far, edge_west], 0)
    close0 = hop_pairs(jnp.where(close_odd, to_west, to_east), 1, 0)
    close1 = hop_pairs(jnp.where(close_odd, to_east, to_west), 1, 1)
    if fsdp_count == 4:
        pieces = [packed, packed_out, packed_core, packed_last]
    else:
        gathered = lax.all_gather(packed, "fsdp")
        pieces = [gathered[i] for i in range(fsdp_count)]

    cells = tiles * side
    part = jax.ShapeDtypeStruct((fsdp_count // 2, 2, share, HALF_SUM), F32)
    dense = pl.pallas_call(
        functools.partial(expand_kernel, chans),
        out_shape=jax.ShapeDtypeStruct((taps * LANES, LANES), BF16),
        in_specs=[VMEM] * len(pieces),
        out_specs=VMEM,
        scratch_shapes=[pltpu.VMEM((2 * HALF_TAPS * GROUP, LANES), F32)],
        compiler_params=pltpu.CompilerParams(vmem_limit_bytes=16 * 1024 * 1024),
        name="expand",
    )(*pieces)
    activations, keep, send = pl.pallas_call(
        main_kernel,
        out_shape=(jax.ShapeDtypeStruct(fields.shape, BF16), part, part),
        in_specs=[SMEM, ANY, ANY] + [VMEM] * 7,
        out_specs=(ANY, VMEM, VMEM),
        scratch_shapes=[
            pltpu.VMEM(fields.shape, BF16),
            pltpu.VMEM(fields.shape, BF16),
            pltpu.VMEM(fields.shape, BF16),
            pltpu.SemaphoreType.DMA((2 + rows // min(STEP, rows),)),
            pltpu.VMEM((4 * tiles + 1, tall, RIM, LANES), F32),
            pltpu.VMEM((4 * tiles + 1, tall, RIM, LANES), F32),
            pltpu.VMEM((2, side, RIM, LANES), F32),
            pltpu.VMEM((tall, tiles, side + 16, LANES), F32),
            pltpu.VMEM((tall, cells, KS * LANES), BF16),
            pltpu.VMEM((tall, KS * XROWS, cells), BF16),
            pltpu.VMEM((rows, cells, LANES), BF16),
            pltpu.VMEM((SUM_LANES, LANES), F32),
            pltpu.VMEM((fsdp_count, share, SUM_LANES), F32),
        ],
        compiler_params=pltpu.CompilerParams(vmem_limit_bytes=46 * 1024 * 1024),
        name="section",
    )(
        neighbours, fields, cotangent, above, below,
        far0, far1, close0, close1, dense,
    )

    held = keep + swapped(send, "fsdp", lambda i: i ^ 1)
    half = space % 2
    distance = 2
    while held.shape[0] > 1:
        pairs = held.reshape(held.shape[0] // 2, 2, 2, share, HALF_SUM)
        sent = narrowed(pairs[:, 1], half)
        held = pairs[:, 0] + swapped(sent, "fsdp", lambda i: i ^ distance).astype(F32)
        distance *= 2
    held = held[0, 0] + swapped(held[0, 1], "space", lambda i: i ^ 1)
    distance = 2
    while distance * 4 < space_count:
        held = held + swapped(held, "space", lambda i: i ^ distance)
        distance *= 2
    rounded = narrowed(jnp.stack([held]), half)[0]
    others = [swapped(rounded, "space", lambda i, k=k: i ^ (distance * k)) for k in (1, 2, 3)]
    total = (rounded.astype(F32) + others[0].astype(F32)) + (
        others[1].astype(F32) + others[2].astype(F32)
    )
    exact = total[:, BIAS_AT : BIAS_AT + 1] + total[:, BIAS_AT + 1 : BIAS_AT + 2]
    total = jnp.where(bias_lane(total.shape, half, BIAS_AT), exact, total)
    total = jnp.where(bias_lane(total.shape, half, BIAS_AT + 1), 0.0, total)
    squares = jnp.broadcast_to(jnp.sum(total * total, 0, keepdims=True), (8, HALF_SUM))
    total_beside = swapped(total, "space", lambda i: i ^ 1)
    distance = 1
    while distance * 2 < fsdp_count:
        squares = squares + swapped(squares, "fsdp", lambda i: i ^ distance)
        distance *= 2
    both = [
        (s * fsdp_count + q, (s ^ 1) * fsdp_count + (q ^ distance))
        for s in range(space_count)
        for q in range(fsdp_count)
    ]
    all_squares = [
        squares,
        swapped(squares, "space", lambda i: i ^ 1),
        swapped(squares, "fsdp", lambda i: i ^ distance),
        lax.ppermute(squares, ("space", "fsdp"), both),
    ]
    weight_step, bias_step = pl.pallas_call(
        functools.partial(scale_kernel, taps * GROUP * chans + chans),
        out_shape=(
            jax.ShapeDtypeStruct((KS, KS, GROUP, share), F32),
            jax.ShapeDtypeStruct((1, share), F32),
        ),
        in_specs=[VMEM] * 6,
        out_specs=(VMEM, VMEM),
        compiler_params=SMALL,
        name="scale",
    )(total, total_beside, *all_squares)
    return (activations, weight_step, bias_step[0])


def solution(mesh):
    return jax.shard_map(
        per_device,
        mesh=mesh,
        in_specs=(
            P("space", "fsdp", None, None),
            P(None, None, None, "fsdp"),
            P("fsdp"),
            P("space", "fsdp", None, None),
            P("space", None),
        ),
        out_specs=(P("space", "fsdp", None, None), P(None, None, None, "fsdp"), P("fsdp")),
        check_vma=False,
    )
```

```python
import functools

import jax
import jax.numpy as jnp
from jax import lax
from jax.experimental import pallas as pl
from jax.experimental.pallas import tpu as pltpu
from jax.sharding import PartitionSpec as P

GROUP = 40
KS = 5
RIM = 2
LANES = 256
HALF = 64
HALF_TAPS = 13
PIECE_ROWS = 528
SUM_LANES = 1024
STEP = 4
HALF_SUM = SUM_LANES // 2
BIAS_AT = KS * KS * GROUP - HALF_SUM
XROWS = 208
VMEM = pl.BlockSpec(memory_space=pltpu.VMEM)
ANY = pl.BlockSpec(memory_space=pl.ANY)
SMEM = pl.BlockSpec(memory_space=pltpu.SMEM)
F32 = jnp.float32
SMALL = pltpu.CompilerParams(vmem_limit_bytes=12 * 1024 * 1024)
BF16 = jnp.bfloat16


def swapped(value, axis, partner):
    count = lax.axis_size(axis)
    pairs = [(i, partner(i)) for i in range(count)]
    return lax.ppermute(value, axis, [p for p in pairs if 0 <= p[1] < count])


def hop_pairs(value, distance, parity):
    def partner(i):
        return i + distance if (i // distance) % 2 == parity else i - distance

    return swapped(value, "space", partner)


def expand_kernel(chans, *refs):
    *pieces, wd, wc = refs
    piece_count = len(pieces)
    fsdp_count = lax.axis_size("fsdp")
    fsdp = lax.axis_index("fsdp")
    share = chans // fsdp_count

    lined = jnp.concatenate([p[...] for p in pieces], axis=1)
    owner = []
    for i in range(piece_count):
        if piece_count == fsdp_count and fsdp_count != 4:
            owner.append(i)
        else:
            owner.append((fsdp, 3 - fsdp, fsdp ^ 1, fsdp ^ 2)[i])
    from_lane = lax.broadcasted_iota(jnp.int32, (128, LANES), 0)
    to_lane = lax.broadcasted_iota(jnp.int32, (128, LANES), 1)
    for half in range(2):
        picks = []
        for i in range(piece_count):
            inside = from_lane - half * HALF
            valid = (inside >= 0) & (inside < share) & (to_lane == owner[i] * share + inside)
            picks.append(jnp.where(valid, 1.0, 0.0).astype(BF16))
        full = jnp.dot(lined, jnp.concatenate(picks, axis=0), preferred_element_type=F32)
        wc[half * HALF_TAPS * GROUP : (half + 1) * HALF_TAPS * GROUP, :] = full[: HALF_TAPS * GROUP]
    group_count = chans // GROUP
    group_of = lax.broadcasted_iota(jnp.int32, (GROUP, LANES), 1) // GROUP
    taps = KS * KS
    for tap in range(taps):
        one = wc[tap * GROUP : (tap + 1) * GROUP]
        blocks = [jnp.where(group_of == k, one, 0.0) for k in range(group_count)]
        if tap == taps // 2:
            blocks.append(wc[taps * GROUP : taps * GROUP + 8])
        else:
            blocks.append(jnp.zeros((8, LANES), F32))
        blocks.append(jnp.zeros((LANES - chans - 8, LANES), F32))
        wd[tap * LANES : (tap + 1) * LANES] = jnp.concatenate(blocks, axis=0).astype(BF16)


def main_kernel(
    near, fields_far, cot_far, above, below, far0, far1, close0, close1, wd,
    act_far, keep, send, fields, cot, act, sems, pool_l, pool_r, edges, xf, xs, xst, g, gd, shares,
):
    fields_in = pltpu.make_async_copy(fields_far, fields, sems.at[0])
    cot_in = pltpu.make_async_copy(cot_far, cot, sems.at[1])
    fields_in.start()
    cot_in.start()
    tiles, rows, side, chans = fields.shape
    tall = rows + 2 * RIM
    cells = tiles * side
    fsdp_count = lax.axis_size("fsdp")
    fsdp = lax.axis_index("fsdp")
    space = lax.axis_index("space")
    far_odd = lax.rem(lax.div(space, 2), 2) == 1
    close_odd = lax.rem(space, 2) == 1
    share = chans // fsdp_count

    group_count = chans // GROUP
    group_of = lax.broadcasted_iota(jnp.int32, (GROUP, LANES), 1) // GROUP
    taps = KS * KS

    zero_side = jnp.zeros((tall, RIM, LANES), F32)
    zero_slot = 4 * tiles
    pool_l[zero_slot] = zero_side
    pool_r[zero_slot] = zero_side
    for t in range(tiles):
        lo, hi = far0[t].astype(F32), far1[t].astype(F32)
        pool_l[tiles + t, :, :, :chans] = jnp.where(far_odd, lo, hi)
        pool_r[2 * tiles + t, :, :, :chans] = jnp.where(far_odd, hi, lo)
        lo = close0[t * tall : (t + 1) * tall].astype(F32)
        hi = close1[t * tall : (t + 1) * tall].astype(F32)
        pool_l[2 * tiles + t, :, :, :chans] = jnp.where(close_odd, lo, hi)
        pool_r[tiles + t, :, :, :chans] = jnp.where(close_odd, hi, lo)
    lo = close0[tiles * tall : tiles * tall + RIM].astype(F32)
    hi = close1[tiles * tall : tiles * tall + RIM].astype(F32)
    pool_l[tiles - 1, :RIM, :, :chans] = jnp.where(close_odd, lo, hi)
    pool_r[3 * tiles, rows + RIM :, :, :chans] = jnp.where(close_odd, hi, lo)

    lo = close0[tiles * tall + RIM :].astype(F32)
    hi = close1[tiles * tall + RIM :].astype(F32)
    edges[0, :, :, :chans] = jnp.where(close_odd, lo, hi)
    edges[1, :, :, :chans] = jnp.where(close_odd, hi, lo)
    edge_north = jnp.stack([edges[0, :, r, :chans] for r in range(RIM)])
    edge_south = jnp.stack([edges[1, :, r, :chans] for r in range(RIM)])
    fields_in.wait()

    lane = lax.broadcasted_iota(jnp.int32, (tiles, side + 16, 128), 2)
    one_behind = jnp.where(lane == chans - 128, 1.0, 0.0).astype(F32)
    for r in range(tall):
        xf[r, :, :, 128:] = one_behind
    for t in range(tiles):
        top, bottom = above[t].astype(F32), below[t].astype(F32)
        centre = fields[t].astype(F32)
        for part, first in ((top, 0), (centre, RIM), (bottom, RIM + rows)):
            length = part.shape[0]
            pool_l[3 * tiles + t, first : first + length, :, :chans] = part[:, side - RIM :]
            pool_r[t, first : first + length, :, :chans] = part[:, :RIM]
        xf[RIM : RIM + rows, t, 8 : 8 + side, :chans] = centre
        north = edge_north if t == 0 else above[t - 1].astype(F32)
        south = edge_south if t == tiles - 1 else below[t + 1].astype(F32)
        north = jnp.where(near[t, 0] >= 0, north, 0.0)
        south = jnp.where(near[t, 1] >= 0, south, 0.0)
        xf[:RIM, t, 8 : 8 + side, :chans] = jnp.where(fsdp == 0, north, top)
        xf[RIM + rows :, t, 8 : 8 + side, :chans] = jnp.where(fsdp == fsdp_count - 1, south, bottom)

    def slot(tile_id, first):
        return jnp.where(tile_id < 0, zero_slot, jnp.clip(tile_id - first * tiles, 0, zero_slot))

    for t in range(tiles):
        for pool, column, first, beside, up, down in (
            (pool_l, 6, space - 3, near[t, 2], near[t, 4], near[t, 6]),
            (pool_r, 8 + side, space, near[t, 3], near[t, 5], near[t, 7]),
        ):
            mid = slot(beside, first)
            top = jnp.where(fsdp == 0, slot(up, first), mid)
            bottom = jnp.where(fsdp == fsdp_count - 1, slot(down, first), mid)
            into = pl.ds(column, RIM)
            xf[RIM : RIM + rows, t, into, :chans] = pool[mid, RIM : RIM + rows, :, :chans]
            xf[:RIM, t, into, :chans] = pool[top, :RIM, :, :chans]
            xf[RIM + rows :, t, into, :chans] = pool[bottom, RIM + rows :, :, :chans]

    def shift(some_rows):
        for r in some_rows:
            for b in range(KS):
                piece = xf[r, :, 6 + b : 6 + b + side, :].astype(BF16).reshape(cells, LANES)
                xs[r, :, b * LANES : (b + 1) * LANES] = piece
                xst[r, b * XROWS : (b + 1) * XROWS, :] = piece.T[:XROWS]

    cot_in.wait()
    act_out = []
    step = min(STEP, rows)
    reach = step + KS - 1
    shift(range(reach))
    for r0 in range(0, rows, step):
        if r0 + step < rows:
            shift(range(r0 + reach, r0 + reach + step))
        total = None
        for a in range(KS):
            left = xs[r0 + a : r0 + a + step].reshape(step * cells, KS * LANES)
            right = wd[a * KS * LANES : (a + 1) * KS * LANES]
            part = jnp.dot(left, right, preferred_element_type=F32)
            total = part if total is None else total + part
        total = total.reshape(step, tiles, side, LANES)
        for t in range(tiles):
            pre = total[:, t, :, :chans]
            logistic = 1.0 / (1.0 + jnp.exp(-pre))
            act[t, r0 : r0 + step] = (pre * logistic).astype(BF16)
            up = cot[t, r0 : r0 + step].astype(F32)
            g[r0 : r0 + step, t * side : (t + 1) * side, :chans] = (
                up * logistic * (1.0 + pre * (1.0 - logistic))
            ).astype(BF16)

        chunk = pl.ds(r0, step)
        act_out.append(
            pltpu.make_async_copy(act.at[:, chunk], act_far.at[:, chunk], sems.at[2 + r0 // step])
        )
        act_out[-1].start()

    right = g[...].reshape(rows * cells, LANES)
    for a in range(KS):
        left = jnp.concatenate([xst[r + a] for r in range(rows)], axis=1)
        part = jnp.dot(left, right, preferred_element_type=F32)
        for b in range(KS):
            fold = jnp.zeros((GROUP, LANES), F32)
            for k in range(group_count):
                first = b * XROWS + k * GROUP
                fold = jnp.where(group_of == k, part[first : first + GROUP], fold)
            first = (a * KS + b) * GROUP
            gd[first : first + GROUP] = fold
        if a == 0:
            gd[taps * GROUP : taps * GROUP + 8] = part[chans : chans + 8]
            gd[taps * GROUP + 8 :] = jnp.zeros((SUM_LANES - taps * GROUP - 8, LANES), F32)
    turned = gd[...].T
    for i in range(fsdp_count):
        shares[i] = turned[i * share : (i + 1) * share]
    for i in range(fsdp_count // 2):
        for into, whose in ((keep, fsdp ^ (2 * i)), (send, fsdp ^ (2 * i + 1))):
            low, high = shares[whose, :, :HALF_SUM], shares[whose, :, HALF_SUM:]
            into[i, 0] = jnp.where(close_odd, high, low)
            into[i, 1] = jnp.where(close_odd, low, high)
    for copy in act_out:
        copy.wait()


def bias_lane(shape, half, at):
    lane = lax.broadcasted_iota(jnp.int32, shape, len(shape) - 1)
    return (lane == at) & (half == 1)


def narrowed(value, half):
    lead = value.shape[:-2]
    index = lax.broadcasted_iota(jnp.int32, value.shape, len(lead) - 1)
    whose = index ^ half
    bias_sum = value[..., BIAS_AT : BIAS_AT + 1] + value[..., BIAS_AT + 1 : BIAS_AT + 2]
    bias_low = bias_sum - lax.reduce_precision(bias_sum, 8, 7)
    value = jnp.where(bias_lane(value.shape, whose, BIAS_AT), bias_sum, value)
    return jnp.where(bias_lane(value.shape, whose, BIAS_AT + 1), bias_low, value).astype(BF16)


def scale_kernel(entries, own, beside, *rest):
    squares, (weight_out, bias_out) = rest[:-2], rest[-2:]
    odd = lax.rem(lax.axis_index("space"), 2) == 1
    count = KS * KS * GROUP
    share = own.shape[0]
    sums = [value[0:1, :] for value in squares]
    while len(sums) > 1:
        sums = [a + b for a, b in zip(sums[::2], sums[1::2])]
    scaling = lax.rsqrt(jnp.sum(sums[0], axis=1, keepdims=True) / entries + 1e-06)
    low = jnp.where(odd, beside[...], own[...])
    high = jnp.where(odd, own[...], beside[...])
    whole = jnp.concatenate([low, high], axis=1) * scaling
    whole = jnp.concatenate([whole, jnp.zeros((128 - share, SUM_LANES), F32)], axis=0)
    turned = whole.T
    weight_out[...] = turned[:count, :share].reshape(weight_out.shape)
    bias_out[...] = turned[count : count + 1, :share]


def rim_kernel(
    fields, ends_outward, ends_core, rows_outward, rows_core, west, east, rims, sides, sems
):
    rows, side = fields.shape[1:3]
    even = lax.rem(lax.axis_index("fsdp"), 2) == 0
    copies = [
        pltpu.make_async_copy(fields.at[:, pl.ds(0, RIM)], rims.at[0], sems.at[0]),
        pltpu.make_async_copy(fields.at[:, pl.ds(rows - RIM, RIM)], rims.at[1], sems.at[1]),
        pltpu.make_async_copy(fields.at[:, :, pl.ds(0, 16)], sides.at[0], sems.at[2]),
        pltpu.make_async_copy(fields.at[:, :, pl.ds(side - 16, 16)], sides.at[1], sems.at[3]),
    ]
    for copy in copies:
        copy.start()
    for copy in copies:
        copy.wait()

    def give(first_ends, first_rows, last_ends, last_rows):
        for i, (ends, outer) in enumerate(((first_ends, first_rows), (last_ends, last_rows))):
            outer[...] = rims[i]
            ends[:, :, :RIM] = rims[i, :, :, :RIM]
            ends[:, :, RIM:] = rims[i, :, :, side - RIM :]

    @pl.when(even)
    def _():
        give(ends_outward, rows_outward, ends_core, rows_core)

    @pl.when(jnp.logical_not(even))
    def _():
        give(ends_core, rows_core, ends_outward, rows_outward)

    west[...] = sides[0, :, :, :RIM]
    east[...] = sides[1, :, :, 16 - RIM :]


def pack_kernel(weight, bias, packed, wide):
    share = weight.shape[2]
    high = KS * KS - HALF_TAPS
    wide[...] = jnp.zeros(wide.shape, F32)
    wide[: HALF_TAPS * GROUP, :share] = weight[:HALF_TAPS].astype(F32).reshape(-1, share)
    wide[: high * GROUP, HALF : HALF + share] = weight[HALF_TAPS:].astype(F32).reshape(-1, share)
    wide[high * GROUP : high * GROUP + 1, HALF : HALF + share] = bias[...].astype(F32)
    packed[...] = wide[...].astype(BF16)


def per_device(fields, weight, bias, cotangent, neighbours):
    tiles, rows, side, chans = fields.shape
    fsdp_count = lax.axis_size("fsdp")
    space_count = lax.axis_size("space")
    fsdp = lax.axis_index("fsdp")
    space = lax.axis_index("space")
    share = chans // fsdp_count
    taps = KS * KS
    tall = rows + 2 * RIM

    even = fsdp % 2 == 0

    def outward(i):
        return (i + 1) % fsdp_count if i % 2 else (i - 1) % fsdp_count

    def joined(name_outward, name_core):
        up = jnp.where(even, name_outward, name_core)
        return up, jnp.where(even, name_core, name_outward)

    def inward(i):
        return i ^ 1

    ends = jax.ShapeDtypeStruct((tiles, RIM, 2 * RIM, chans), BF16)
    rim = jax.ShapeDtypeStruct((tiles, RIM, side, chans), BF16)
    columns = jax.ShapeDtypeStruct((tiles, rows, RIM, chans), BF16)
    ends_outward, ends_core, rows_outward, rows_core, west_own, east_own = pl.pallas_call(
        rim_kernel,
        out_shape=(ends, ends, rim, rim, columns, columns),
        in_specs=[ANY],
        out_specs=(VMEM,) * 6,
        scratch_shapes=[
            pltpu.VMEM((2, tiles, RIM, side, chans), BF16),
            pltpu.VMEM((2, tiles, rows, 16, chans), BF16),
            pltpu.SemaphoreType.DMA((4,)),
        ],
        compiler_params=SMALL,
        name="rims",
    )(fields)
    packed = pl.pallas_call(
        pack_kernel,
        out_shape=jax.ShapeDtypeStruct((PIECE_ROWS, 128), BF16),
        in_specs=[VMEM] * 2,
        out_specs=VMEM,
        scratch_shapes=[pltpu.VMEM((PIECE_ROWS, 128), F32)],
        compiler_params=SMALL,
        name="pack",
    )(weight.reshape(taps, GROUP, share), bias[None, :])
    ends_outward = swapped(ends_outward, "fsdp", outward)
    ends_core = swapped(ends_core, "fsdp", inward)
    from_outward = swapped(rows_outward, "fsdp", outward)
    from_core = swapped(rows_core, "fsdp", inward)
    if fsdp_count == 4:
        packed_out = swapped(packed, "fsdp", outward)
        packed_core = swapped(packed, "fsdp", inward)
    ends_above, ends_below = joined(ends_outward, ends_core)

    west = jnp.concatenate([ends_above[:, :, :RIM], west_own, ends_below[:, :, :RIM]], 1)
    east = jnp.concatenate([ends_above[:, :, RIM:], east_own, ends_below[:, :, RIM:]], 1)
    far_odd = (space // 2) % 2 == 1
    close_odd = space % 2 == 1
    far0 = hop_pairs(jnp.where(far_odd, west, east), 2, 0)
    far1 = hop_pairs(jnp.where(far_odd, east, west), 2, 1)
    if fsdp_count == 4:
        far0, far1, packed_out = lax.optimization_barrier((far0, far1, packed_out))
        packed_last = swapped(packed_out, "fsdp", inward)
    far0, far1, from_outward, from_core = lax.optimization_barrier(
        (far0, far1, from_outward, from_core)
    )
    above, below = joined(from_outward, from_core)
    east_far = jnp.where(far_odd, far0, far1)[tiles - 1, :RIM]
    west_far = jnp.where(far_odd, far1, far0)[0, rows + RIM :]
    flat_side = (tiles * tall, RIM, chans)
    edge_east = jnp.swapaxes(above[tiles - 1], 0, 1)
    edge_west = jnp.swapaxes(below[0], 0, 1)
    to_east = jnp.concatenate([east.reshape(flat_side), east_far, edge_east], 0)
    to_west = jnp.concatenate([west.reshape(flat_side), west_far, edge_west], 0)
    close0 = hop_pairs(jnp.where(close_odd, to_west, to_east), 1, 0)
    close1 = hop_pairs(jnp.where(close_odd, to_east, to_west), 1, 1)
    if fsdp_count == 4:
        pieces = [packed, packed_out, packed_core, packed_last]
    else:
        gathered = lax.all_gather(packed, "fsdp")
        pieces = [gathered[i] for i in range(fsdp_count)]

    cells = tiles * side
    part = jax.ShapeDtypeStruct((fsdp_count // 2, 2, share, HALF_SUM), F32)
    dense = pl.pallas_call(
        functools.partial(expand_kernel, chans),
        out_shape=jax.ShapeDtypeStruct((taps * LANES, LANES), BF16),
        in_specs=[VMEM] * len(pieces),
        out_specs=VMEM,
        scratch_shapes=[pltpu.VMEM((2 * HALF_TAPS * GROUP, LANES), F32)],
        compiler_params=pltpu.CompilerParams(vmem_limit_bytes=16 * 1024 * 1024),
        name="expand",
    )(*pieces)
    activations, keep, send = pl.pallas_call(
        main_kernel,
        out_shape=(jax.ShapeDtypeStruct(fields.shape, BF16), part, part),
        in_specs=[SMEM, ANY, ANY] + [VMEM] * 7,
        out_specs=(ANY, VMEM, VMEM),
        scratch_shapes=[
            pltpu.VMEM(fields.shape, BF16),
            pltpu.VMEM(fields.shape, BF16),
            pltpu.VMEM(fields.shape, BF16),
            pltpu.SemaphoreType.DMA((2 + rows // min(STEP, rows),)),
            pltpu.VMEM((4 * tiles + 1, tall, RIM, LANES), F32),
            pltpu.VMEM((4 * tiles + 1, tall, RIM, LANES), F32),
            pltpu.VMEM((2, side, RIM, LANES), F32),
            pltpu.VMEM((tall, tiles, side + 16, LANES), F32),
            pltpu.VMEM((tall, cells, KS * LANES), BF16),
            pltpu.VMEM((tall, KS * XROWS, cells), BF16),
            pltpu.VMEM((rows, cells, LANES), BF16),
            pltpu.VMEM((SUM_LANES, LANES), F32),
            pltpu.VMEM((fsdp_count, share, SUM_LANES), F32),
        ],
        compiler_params=pltpu.CompilerParams(vmem_limit_bytes=46 * 1024 * 1024),
        name="section",
    )(
        neighbours, fields, cotangent, above, below,
        far0, far1, close0, close1, dense,
    )

    held = keep + swapped(send, "fsdp", lambda i: i ^ 1)
    half = space % 2
    distance = 2
    while held.shape[0] > 1:
        pairs = held.reshape(held.shape[0] // 2, 2, 2, share, HALF_SUM)
        sent = narrowed(pairs[:, 1], half)
        held = pairs[:, 0] + swapped(sent, "fsdp", lambda i: i ^ distance).astype(F32)
        distance *= 2
    sent = narrowed(jnp.stack([held[0, 1]]), half ^ 1)[0]
    held = held[0, 0] + swapped(sent, "space", lambda i: i ^ 1).astype(F32)
    distance = 2
    while distance * 4 < space_count:
        held = held + swapped(held, "space", lambda i: i ^ distance)
        distance *= 2
    rounded = narrowed(jnp.stack([held]), half)[0]
    others = [swapped(rounded, "space", lambda i, k=k: i ^ (distance * k)) for k in (1, 2, 3)]
    total = (rounded.astype(F32) + others[0].astype(F32)) + (
        others[1].astype(F32) + others[2].astype(F32)
    )
    exact = total[:, BIAS_AT : BIAS_AT + 1] + total[:, BIAS_AT + 1 : BIAS_AT + 2]
    total = jnp.where(bias_lane(total.shape, half, BIAS_AT), exact, total)
    total = jnp.where(bias_lane(total.shape, half, BIAS_AT + 1), 0.0, total)
    squares = jnp.broadcast_to(jnp.sum(total * total, 0, keepdims=True), (8, HALF_SUM))
    total_beside = swapped(total, "space", lambda i: i ^ 1)
    distance = 1
    while distance * 2 < fsdp_count:
        squares = squares + swapped(squares, "fsdp", lambda i: i ^ distance)
        distance *= 2
    both = [
        (s * fsdp_count + q, (s ^ 1) * fsdp_count + (q ^ distance))
        for s in range(space_count)
        for q in range(fsdp_count)
    ]
    all_squares = [
        squares,
        swapped(squares, "space", lambda i: i ^ 1),
        swapped(squares, "fsdp", lambda i: i ^ distance),
        lax.ppermute(squares, ("space", "fsdp"), both),
    ]
    weight_step, bias_step = pl.pallas_call(
        functools.partial(scale_kernel, taps * GROUP * chans + chans),
        out_shape=(
            jax.ShapeDtypeStruct((KS, KS, GROUP, share), F32),
            jax.ShapeDtypeStruct((1, share), F32),
        ),
        in_specs=[VMEM] * 6,
        out_specs=(VMEM, VMEM),
        compiler_params=SMALL,
        name="scale",
    )(total, total_beside, *all_squares)
    return (activations, weight_step, bias_step[0])


def solution(mesh):
    return jax.shard_map(
        per_device,
        mesh=mesh,
        in_specs=(
            P("space", "fsdp", None, None),
            P(None, None, None, "fsdp"),
            P("fsdp"),
            P("space", "fsdp", None, None),
            P("space", None),
        ),
        out_specs=(P("space", "fsdp", None, None), P(None, None, None, "fsdp"), P("fsdp")),
        check_vma=False,
    )
```
